32 devices in a mesh: dp: 4 (over x, core), fsdp: 8 (over z, y).
Axes of the slice: x: 2, y: 2, z: 4, core: 2. Of those that a mesh axis runs over, the one named last changes fastest.
Arguments:
- latent: float32 [32, 320, 64], P(('dp', 'fsdp')), may hold values from -20 to 20
- noise: float32 [32, 320, 64], P(('dp', 'fsdp')), may hold values from -6 to 6
- text: bfloat16 [32, 128, 768], P(('dp', 'fsdp')), may hold values from -6 to 6
- steps: int32 [32], P(('dp', 'fsdp')), may hold values from 0 to 7
- empty: int32 [32], P(('dp', 'fsdp')), may hold values 0 or 1
- negatives: int32 [32, 15], P(('dp', 'fsdp')), may hold values from 0 to 31
- latent_in: float32 [64, 1536], P(None, ('dp', 'fsdp')), may hold values from -0.75 to 0.75
- time_proj: float32 [256, 1536], P(('dp', 'fsdp')), may hold values from -0.375 to 0.375
- text_proj: float32 [768, 1536], P(('dp', 'fsdp')), may hold values from -0.21875 to 0.21875
- attn_qkv: float32 [1536, 4608], P(('dp', 'fsdp')), may hold values from -0.15625 to 0.15625
- attn_out: float32 [1536, 1536], P(('dp', 'fsdp')), may hold values from -0.15625 to 0.15625
- glu_in: float32 [1536, 12288], P(('dp', 'fsdp')), may hold values from -0.15625 to 0.15625
- glu_out: float32 [6144, 1536], P(('dp', 'fsdp')), may hold values from -0.078125 to 0.078125
- latent_out: float32 [1536, 64], P(('dp', 'fsdp')), may hold values from -0.3125 to 0.3125
- norm_gains: float32 [3, 1536], P(None, ('dp', 'fsdp')), may hold values from 0.5 to 1.5
- first_latent_in: float32 [64, 1536], P(None, ('dp', 'fsdp')), may hold values from -1.1444092e-05 to 1.1444092e-05
- first_time_proj: float32 [256, 1536], P(('dp', 'fsdp')), may hold values from -2.2888184e-05 to 2.2888184e-05
- first_text_proj: float32 [768, 1536], P(('dp', 'fsdp')), may hold values from -2.2888184e-05 to 2.2888184e-05
- first_attn_qkv: float32 [1536, 4608], P(('dp', 'fsdp')), may hold values from -1.9073486e-06 to 1.9073486e-06
- first_attn_out: float32 [1536, 1536], P(('dp', 'fsdp')), may hold values from -3.8146973e-06 to 3.8146973e-06
- first_glu_in: float32 [1536, 12288], P(('dp', 'fsdp')), may hold values from -1.66893e-06 to 1.66893e-06
- first_glu_out: float32 [6144, 1536], P(('dp', 'fsdp')), may hold values from -3.8146973e-06 to 3.8146973e-06
- first_latent_out: float32 [1536, 64], P(('dp', 'fsdp')), may hold values from -1.5258789e-05 to 1.5258789e-05
- first_norm_gains: float32 [3, 1536], P(None, ('dp', 'fsdp')), may hold values from -5.722046e-06 to 5.722046e-06
- second_latent_in: float32 [64, 1536], P(None, ('dp', 'fsdp')), may hold values from 6.5784786e-12 to 2.6566933e-11
- second_time_proj: float32 [256, 1536], P(('dp', 'fsdp')), may hold values from 2.6566933e-11 to 1.0626773e-10
- second_text_proj: float32 [768, 1536], P(('dp', 'fsdp')), may hold values from 2.6566933e-11 to 1.0626773e-10
- second_attn_qkv: float32 [1536, 4608], P(('dp', 'fsdp')), may hold values from 2.6819953e-13 to 1.0626773e-12
- second_attn_out: float32 [1536, 1536], P(('dp', 'fsdp')), may hold values from 8.096589e-13 to 3.2892393e-12
- second_glu_in: float32 [1536, 12288], P(('dp', 'fsdp')), may hold values from 1.4928086e-13 to 6.072442e-13
- second_glu_out: float32 [6144, 1536], P(('dp', 'fsdp')), may hold values from 9.361681e-13 to 3.7446725e-12
- second_latent_out: float32 [1536, 64], P(('dp', 'fsdp')), may hold values from 1.4928087e-11 to 6.072442e-11
- second_norm_gains: float32 [3, 1536], P(None, ('dp', 'fsdp')), may hold values from 1.6699215e-12 to 6.5784786e-12
Outputs:
- loss_sum: float32 [], replicated
- bucket_sums: float32 [8], replicated
- grad_norm: float32 [], replicated
- new_latent_in: float32 [64, 1536], P(None, ('dp', 'fsdp'))
- new_time_proj: float32 [256, 1536], P(('dp', 'fsdp'))
- new_text_proj: float32 [768, 1536], P(('dp', 'fsdp'))
- new_attn_qkv: float32 [1536, 4608], P(('dp', 'fsdp'))
- new_attn_out: float32 [1536, 1536], P(('dp', 'fsdp'))
- new_glu_in: float32 [1536, 12288], P(('dp', 'fsdp'))
- new_glu_out: float32 [6144, 1536], P(('dp', 'fsdp'))
- new_latent_out: float32 [1536, 64], P(('dp', 'fsdp'))
- new_norm_gains: float32 [3, 1536], P(None, ('dp', 'fsdp'))
- new_first_latent_in: float32 [64, 1536], P(None, ('dp', 'fsdp'))
- new_first_time_proj: float32 [256, 1536], P(('dp', 'fsdp'))
- new_first_text_proj: float32 [768, 1536], P(('dp', 'fsdp'))
- new_first_attn_qkv: float32 [1536, 4608], P(('dp', 'fsdp'))
- new_first_attn_out: float32 [1536, 1536], P(('dp', 'fsdp'))
- new_first_glu_in: float32 [1536, 12288], P(('dp', 'fsdp'))
- new_first_glu_out: float32 [6144, 1536], P(('dp', 'fsdp'))
- new_first_latent_out: float32 [1536, 64], P(('dp', 'fsdp'))
- new_first_norm_gains: float32 [3, 1536], P(None, ('dp', 'fsdp'))
- new_second_latent_in: float32 [64, 1536], P(None, ('dp', 'fsdp'))
- new_second_time_proj: float32 [256, 1536], P(('dp', 'fsdp'))
- new_second_text_proj: float32 [768, 1536], P(('dp', 'fsdp'))
- new_second_attn_qkv: float32 [1536, 4608], P(('dp', 'fsdp'))
- new_second_attn_out: float32 [1536, 1536], P(('dp', 'fsdp'))
- new_second_glu_in: float32 [1536, 12288], P(('dp', 'fsdp'))
- new_second_glu_out: float32 [6144, 1536], P(('dp', 'fsdp'))
- new_second_latent_out: float32 [1536, 64], P(('dp', 'fsdp'))
- new_second_norm_gains: float32 [3, 1536], P(None, ('dp', 'fsdp'))
The draws below stay inside these ranges and needn't reach their ends.
All inputs are finite; a program needn't handle non-finite values. No bound on the sum of `empty` on one device may be relied on, other than what follows from the above.
Results may differ from the reference program's by a relative error of at most 0.003.
The reference program's roundings to bfloat16 on the way (of `qkv`) count: a program that leaves them out, or rounds other values in their place, can miss the bound.
Values may be sent and summed in bfloat16 or wider, within the bound.
A program may use at most 384 MiB of HBM per device.

```python
import math
import jax
import jax.numpy as jnp
from jax import lax

D = 1536
H = 24
HD = 64
FF = 6144
E = 768
TEXT = 128
C = 64
TF = 256
FRAMES = 320
NB = 8
NEG = 15
STEP = 10
CLIPS = 32
NPARAM = 39522816


def draw_latent(key, part):
    key = jax.random.fold_in(key, 7)
    rise = jnp.arange(CLIPS, dtype=jnp.float32)[:, None, None] / max(CLIPS - 1, 1)
    base = jnp.clip(jax.random.normal(key, (CLIPS, FRAMES, C), jnp.float32), -5.0, 5.0)
    return base * (0.5 + 3.5 * rise)


def touch_ends(entries, stream_key, least, top_value):
    longest = entries.shape.index(max(entries.shape))
    spots = []
    for shift in (0, 1):
        where = [jax.random.randint(jax.random.fold_in(stream_key, axis), (), 0, length) for axis, length in enumerate(entries.shape)]
        where[longest] = (where[longest] + shift) % entries.shape[longest]
        spots.append(tuple(where))
    return entries.at[spots[0]].set(least).at[spots[1]].set(top_value)


def shard_levels(stream_key, shape, pieces, low, high):
    def one(position, parts):
        heights = jax.random.uniform(jax.random.fold_in(jax.random.fold_in(stream_key, 6), position), (parts,), jnp.float32, low / len(pieces), high / len(pieces))
        return jnp.repeat(jnp.exp(heights), shape[position] // parts).reshape((-1,) + (1,) * (len(shape) - position - 1))

    level = one(*pieces[0])
    for cut in pieces[1:]:
        level = level * one(*cut)
    return level


def bell_draw(key, extent, width, most, pieces=(), kind=jnp.bfloat16):
    array = width * jax.random.normal(key, extent, jnp.float32)
    if pieces:
        array = array * shard_levels(key, extent, pieces, -0.22, 0.18)
    return jnp.clip(array, -most, most).astype(kind)


def setup_inputs(seed: int = 0) -> dict:
    splits = jax.random.split(jax.random.key(seed), 34)
    latent = draw_latent(jax.random.fold_in(splits[33], 71), 0)
    noise = bell_draw(splits[1], (CLIPS, FRAMES, C), 1.0, 6.0, ((0, 32),), jnp.float32)
    text = bell_draw(splits[2], (CLIPS, TEXT, E), 1.0, 6.0, ((0, 32),))
    steps = touch_ends(jax.random.randint(splits[3], (CLIPS,), 0, NB), jax.random.fold_in(splits[3], 1), 0, NB - 1).astype(jnp.int32)
    empty = touch_ends((jax.random.randint(splits[4], (CLIPS,), 0, 8) < 1).astype(jnp.int32), jax.random.fold_in(splits[4], 1), 0, 1)
    negatives = touch_ends(jax.random.randint(splits[5], (CLIPS, NEG), 0, CLIPS), jax.random.fold_in(splits[5], 1), 0, CLIPS - 1).astype(jnp.int32)
    latent_in = bell_draw(splits[6], (C, D), C ** -0.5, 0.75, ((1, 32),), jnp.float32)
    time_proj = bell_draw(splits[7], (TF, D), TF ** -0.5, 0.375, ((0, 32),), jnp.float32)
    text_proj = bell_draw(splits[8], (E, D), E ** -0.5, 0.21875, ((0, 32),), jnp.float32)
    attn_qkv = bell_draw(splits[9], (D, 3 * D), D ** -0.5, 0.15625, ((0, 32),), jnp.float32)
    attn_out = bell_draw(splits[10], (D, D), D ** -0.5, 0.15625, ((0, 32),), jnp.float32)
    glu_in = bell_draw(splits[11], (D, 2 * FF), D ** -0.5, 0.15625, ((0, 32),), jnp.float32)
    glu_out = bell_draw(splits[12], (FF, D), FF ** -0.5, 0.078125, ((0, 32),), jnp.float32)
    latent_out = bell_draw(splits[13], (D, C), (D // 4) ** -0.5, 0.3125, ((0, 32),), jnp.float32)
    norm_gains = jnp.clip(1.0 + 0.1 * jax.random.normal(splits[14], (3, D), jnp.float32), 0.5, 1.5)
    first_latent_in = bell_draw(splits[15], (C, D), (0.0112 / NPARAM ** 0.5), 1.1444091796875e-05, ((1, 32),), jnp.float32)
    first_time_proj = bell_draw(splits[16], (TF, D), (0.0224 / NPARAM ** 0.5), 2.288818359375e-05, ((0, 32),), jnp.float32)
    first_text_proj = bell_draw(splits[17], (E, D), (0.0224 / NPARAM ** 0.5), 2.288818359375e-05, ((0, 32),), jnp.float32)
    first_attn_qkv = bell_draw(splits[18], (D, 3 * D), (0.0022 / NPARAM ** 0.5), 1.9073486328125e-06, ((0, 32),), jnp.float32)
    first_attn_out = bell_draw(splits[19], (D, D), (0.0039 / NPARAM ** 0.5), 3.814697265625e-06, ((0, 32),), jnp.float32)
    first_glu_in = bell_draw(splits[20], (D, 2 * FF), (0.0017 / NPARAM ** 0.5), 1.6689300537109375e-06, ((0, 32),), jnp.float32)
    first_glu_out = bell_draw(splits[21], (FF, D), (0.0042 / NPARAM ** 0.5), 3.814697265625e-06, ((0, 32),), jnp.float32)
    first_latent_out = bell_draw(splits[22], (D, C), (0.0168 / NPARAM ** 0.5), 1.52587890625e-05, ((0, 32),), jnp.float32)
    first_norm_gains = bell_draw(splits[23], (3, D), (0.0056 / NPARAM ** 0.5), 5.7220458984375e-06, ((1, 32),), jnp.float32)
    second_latent_in = jnp.clip(jnp.exp(math.log(2.656693268154875e-11) - 1.3958638 * jax.random.uniform(splits[24], (C, D), jnp.float32) ** shard_levels(splits[24], (C, D), ((1, 32),), -0.2, 0.2)), 6.578478647240038e-12, 2.656693268154875e-11)
    second_time_proj = jnp.clip(jnp.exp(math.log(1.06267730726195e-10) - 1.3862944 * jax.random.uniform(splits[25], (TF, D), jnp.float32) ** shard_levels(splits[25], (TF, D), ((0, 32),), -0.2, 0.2)), 2.656693268154875e-11, 1.06267730726195e-10)
    second_text_proj = jnp.clip(jnp.exp(math.log(1.06267730726195e-10) - 1.3862944 * jax.random.uniform(splits[26], (E, D), jnp.float32) ** shard_levels(splits[26], (E, D), ((0, 32),), -0.2, 0.2)), 2.656693268154875e-11, 1.06267730726195e-10)
    second_attn_qkv = jnp.clip(jnp.exp(math.log(1.0626772899147152e-12) - 1.3768155 * jax.random.uniform(splits[27], (D, 3 * D), jnp.float32) ** shard_levels(splits[27], (D, 3 * D), ((0, 32),), -0.2, 0.2)), 2.6819952508860823e-13, 1.0626772899147152e-12)
    second_attn_out = jnp.clip(jnp.exp(math.log(3.289239323620019e-12) - 1.4017985 * jax.random.uniform(splits[28], (D, D), jnp.float32) ** shard_levels(splits[28], (D, D), ((0, 32),), -0.2, 0.2)), 8.096589262755749e-13, 3.289239323620019e-12)
    second_glu_in = jnp.clip(jnp.exp(math.log(6.07244181154154e-13) - 1.40310151 * jax.random.uniform(splits[29], (D, 2 * FF), jnp.float32) ** shard_levels(splits[29], (D, 2 * FF), ((0, 32),), -0.2, 0.2)), 1.4928085623113624e-13, 6.07244181154154e-13)
    second_glu_out = jnp.clip(jnp.exp(math.log(3.7446725408007975e-12) - 1.3862944 * jax.random.uniform(splits[30], (FF, D), jnp.float32) ** shard_levels(splits[30], (FF, D), ((0, 32),), -0.2, 0.2)), 9.361681352001994e-13, 3.7446725408007975e-12)
    second_latent_out = jnp.clip(jnp.exp(math.log(6.072441854909627e-11) - 1.4031015 * jax.random.uniform(splits[31], (D, C), jnp.float32) ** shard_levels(splits[31], (D, C), ((0, 32),), -0.2, 0.2)), 1.492808654468547e-11, 6.072441854909627e-11)
    second_norm_gains = jnp.clip(jnp.exp(math.log(6.578478647240038e-12) - 1.3710269 * jax.random.uniform(splits[32], (3, D), jnp.float32) ** shard_levels(splits[32], (3, D), ((1, 32),), -0.2, 0.2)), 1.6699214710688692e-12, 6.578478647240038e-12)
    return dict(latent=latent, noise=noise, text=text, steps=steps, empty=empty, negatives=negatives, latent_in=latent_in, time_proj=time_proj, text_proj=text_proj, attn_qkv=attn_qkv, attn_out=attn_out, glu_in=glu_in, glu_out=glu_out, latent_out=latent_out, norm_gains=norm_gains, first_latent_in=first_latent_in, first_time_proj=first_time_proj, first_text_proj=first_text_proj, first_attn_qkv=first_attn_qkv, first_attn_out=first_attn_out, first_glu_in=first_glu_in, first_glu_out=first_glu_out, first_latent_out=first_latent_out, first_norm_gains=first_norm_gains, second_latent_in=second_latent_in, second_time_proj=second_time_proj, second_text_proj=second_text_proj, second_attn_qkv=second_attn_qkv, second_attn_out=second_attn_out, second_glu_in=second_glu_in, second_glu_out=second_glu_out, second_latent_out=second_latent_out, second_norm_gains=second_norm_gains)


@jax.custom_vjp
def low(v):
    return lax.optimization_barrier(v.astype(jnp.bfloat16)).astype(jnp.float32)

@jax.custom_vjp
def low_back(v):
    return v

def low_keep(v):
    return (low(v), None)

def low_pass(kept, grad):
    return (grad,)

def back_keep(v):
    return (v, None)

def back_low(kept, grad):
    return (low(grad),)
low.defvjp(low_keep, low_pass)
low_back.defvjp(back_keep, back_low)
EPS_NORM = 1e-05
BETA_ONE = 0.9
BETA_TWO = 0.95
ADAM_EPS = 1e-08
RATE = 0.02
GAIN_RATE = 0.3
DECAY = 0.01
CLIP_NORM = 0.05
CON_WEIGHT = 0.5
INV_TEMP = 50.0
HIGH = lax.Precision.HIGHEST

def matmul(left, right):
    return jnp.dot(left, right, precision=HIGH)

def layer_norm(x, gain):
    cent = x - lax.optimization_barrier(jnp.mean(x, axis=-1, keepdims=True))
    var = lax.optimization_barrier(jnp.mean(cent * cent, axis=-1, keepdims=True))
    return cent * lax.rsqrt(var + EPS_NORM) * gain

def unit_scale(x):
    return x * lax.rsqrt(jnp.mean(x * x) + EPS_NORM)

def time_features(step_id):
    place = (step_id.astype(jnp.float32) + 0.5) / NB
    half = TF // 2
    freqs = jnp.exp(jnp.arange(half, dtype=jnp.float32) * (math.log(100.0) / half))
    angle = place * freqs
    return jnp.concatenate([jnp.cos(angle), jnp.sin(angle)])

def clip_terms(params, latent, noise, text, step_id, flag):
    lat_w, time_w, text_w, qkv_w, out_w, gu_w, down_w, lout_w, gains = params
    place = (step_id.astype(jnp.float32) + 0.5) / NB
    alpha = jnp.cos(0.5 * jnp.pi * place)
    sigma = jnp.sin(0.5 * jnp.pi * place)
    noisy = alpha * latent + sigma * noise
    target = alpha * noise - sigma * latent
    feats = time_features(step_id)
    frames = low_back(matmul(low(noisy), lat_w) + matmul(low(feats)[None], time_w))
    words = low_back(matmul(text, text_w))
    hidden = jnp.concatenate([frames, words], 0)
    seq = FRAMES + TEXT
    qkv = low(low_back(matmul(low(layer_norm(hidden, gains[0])), qkv_w)))
    query = qkv[:, :D].reshape(seq, H, HD)
    keys = qkv[:, D:2 * D].reshape(seq, H, HD)
    values = qkv[:, 2 * D:].reshape(seq, H, HD)
    scores = low_back(jnp.einsum('qhd,khd->hqk', query, keys, precision=HIGH) * HD ** (-0.5))
    keep = (jnp.arange(seq) < FRAMES) | (flag == 0)
    scores = jnp.where(keep[None, None, :], scores, -1e+30)
    probs = jax.nn.softmax(scores, axis=-1)
    mixed = low_back(jnp.einsum('hqk,khd->qhd', low(probs), values, precision=HIGH).reshape(seq, D))
    after = hidden + low_back(matmul(low(mixed), out_w))
    gate_up = low(low_back(matmul(low(layer_norm(after, gains[1])), gu_w)))
    inner = low(jax.nn.silu(gate_up[:, :FF]) * gate_up[:, FF:])
    final = after + low_back(matmul(inner, down_w))
    audio = final[:FRAMES]
    pred = low_back(matmul(low(layer_norm(audio, gains[2])), lout_w))
    error = pred - target
    mse = jnp.sum(error * error) / (FRAMES * C)
    return (mse, unit_scale(lax.optimization_barrier(jnp.mean(audio, 0))), unit_scale(lax.optimization_barrier(jnp.mean(words, 0))))

def total_loss(params, latent, noise, text, steps, empty, negatives):
    low_params = tuple((low(p) for p in params))

    def one(items):
        return clip_terms(low_params, *items)
    mse, audio_vec, text_vec = lax.map(jax.checkpoint(one), (latent, noise, text, steps, empty))
    sent = low(text_vec)
    picks = jnp.concatenate([jnp.arange(CLIPS, dtype=jnp.int32)[:, None], negatives.astype(jnp.int32)], 1)
    rows = sent[picks]
    sims = INV_TEMP / D * jnp.einsum('cd,cjd->cj', audio_vec, rows, precision=HIGH)
    con = jax.nn.logsumexp(sims, axis=1) - sims[:, 0]
    weight = CON_WEIGHT * (1 - empty).astype(jnp.float32)
    per_clip = mse + weight * con
    return (jnp.sum(per_clip), mse)

def reference(latent, noise, text, steps, empty, negatives, latent_in, time_proj, text_proj, attn_qkv, attn_out, glu_in, glu_out, latent_out, norm_gains, first_latent_in, first_time_proj, first_text_proj, first_attn_qkv, first_attn_out, first_glu_in, first_glu_out, first_latent_out, first_norm_gains, second_latent_in, second_time_proj, second_text_proj, second_attn_qkv, second_attn_out, second_glu_in, second_glu_out, second_latent_out, second_norm_gains):
    params = (latent_in, time_proj, text_proj, attn_qkv, attn_out, glu_in, glu_out, latent_out, norm_gains)
    firsts = (first_latent_in, first_time_proj, first_text_proj, first_attn_qkv, first_attn_out, first_glu_in, first_glu_out, first_latent_out, first_norm_gains)
    seconds = (second_latent_in, second_time_proj, second_text_proj, second_attn_qkv, second_attn_out, second_glu_in, second_glu_out, second_latent_out, second_norm_gains)
    words = text.astype(jnp.float32)

    def objective(*weights):
        return total_loss(weights, latent, noise, words, steps, empty, negatives)
    loss_sum, pull, mse = jax.vjp(objective, *params, has_aux=True)
    grads = pull(jnp.ones_like(loss_sum))
    bucket_sums = lax.optimization_barrier(jnp.sum(jnp.where(steps[:, None] == jnp.arange(NB, dtype=jnp.int32)[None, :], mse[:, None], 0.0), 0))
    squares = jnp.zeros((), loss_sum.dtype)
    for grad in grads:
        squares = squares + jnp.sum(grad * grad)
    grad_norm = jnp.sqrt(squares)
    scale = jnp.minimum(1.0, CLIP_NORM / (grad_norm + 1e-06))
    new_weights, new_firsts, new_seconds = ([], [], [])
    for index, (weight, first, second, grad) in enumerate(zip(params, firsts, seconds, grads)):
        rate = GAIN_RATE if index == len(params) - 1 else RATE
        grad = grad * scale
        first = BETA_ONE * first + (1.0 - BETA_ONE) * grad
        second = BETA_TWO * second + (1.0 - BETA_TWO) * grad * grad
        fixed_first = first / (1.0 - BETA_ONE ** STEP)
        fixed_second = second / (1.0 - BETA_TWO ** STEP)
        weight = weight - rate * (fixed_first / (jnp.sqrt(fixed_second) + ADAM_EPS) + DECAY * weight)
        new_weights.append(weight)
        new_firsts.append(first)
        new_seconds.append(second)
    return (loss_sum, bucket_sums, grad_norm, new_weights[0], new_weights[1], new_weights[2], new_weights[3], new_weights[4], new_weights[5], new_weights[6], new_weights[7], new_weights[8], new_firsts[0], new_firsts[1], new_firsts[2], new_firsts[3], new_firsts[4], new_firsts[5], new_firsts[6], new_firsts[7], new_firsts[8], new_seconds[0], new_seconds[1], new_seconds[2], new_seconds[3], new_seconds[4], new_seconds[5], new_seconds[6], new_seconds[7], new_seconds[8])
```

```python
import functools
import math

import jax
import jax.numpy as jnp
from jax import lax
from jax.experimental import pallas as pl
from jax.experimental.pallas import tpu as pltpu
from jax.sharding import PartitionSpec as P

AXES = ("dp", "fsdp")
MESH = pl.DeviceIdType.MESH
LANES = 128

HD = 64
TF = 256
NB = 8
STEP = 10


EPS_NORM = 1e-05
BETA_ONE = 0.9
BETA_TWO = 0.95
ADAM_EPS = 1e-08
RATE = 0.02
GAIN_RATE = 0.3
DECAY = 0.01
CLIP_NORM = 0.05
CON_WEIGHT = 0.5
INV_TEMP = 50.0
HIGH = lax.Precision.HIGHEST


def matmul(left, right):
    return jnp.dot(left, right, preferred_element_type=jnp.float32)


def matmul_tn(left, right):
    return lax.dot_general(
        left, right, (((0,), (0,)), ((), ())), preferred_element_type=jnp.float32
    )


def matmul_nt(left, right):
    return lax.dot_general(
        left, right, (((1,), (1,)), ((), ())), preferred_element_type=jnp.float32
    )


def layer_norm(x, gain):
    cent = x - jnp.mean(x, axis=-1, keepdims=True)
    var = jnp.mean(cent * cent, axis=-1, keepdims=True)
    return cent * lax.rsqrt(var + EPS_NORM) * gain


def norm_back(x, gain, grad):
    _, pull = jax.vjp(layer_norm, x, gain)
    return pull(grad)


def unit_scale(x):
    return x * lax.rsqrt(jnp.mean(x * x) + EPS_NORM)


def time_features(step_id):
    place = (step_id.astype(jnp.float32) + 0.5) / NB
    half = TF // 2
    freqs = jnp.exp(jnp.arange(half, dtype=jnp.float32) * (math.log(100.0) / half))
    angle = place * freqs
    return jnp.concatenate([jnp.cos(angle), jnp.sin(angle)])


def attention_probs(query, keys, keep, lse_rows):
    scores = jnp.einsum("qhd,khd->hqk", query, keys, preferred_element_type=jnp.float32) * HD ** (
        -0.5
    )
    scores = jnp.where(keep[None, None, :], scores, -1e30)
    if lse_rows is None:
        top = jnp.max(scores, axis=-1, keepdims=True)
        lse_rows = top + jnp.log(jnp.sum(jnp.exp(scores - top), axis=-1, keepdims=True))
    return (jnp.exp(scores - lse_rows), lse_rows)


def layer_forward(weights, noisy, feats, words_in, flag):
    lat_w, time_w, text_w, qkv_w, out_w, gu_w, down_w, lout_w, gains = weights
    gains = gains.astype(jnp.float32)
    frame_n = noisy.shape[0]
    noisy_b = noisy.astype(jnp.bfloat16)
    feats_b = feats.astype(jnp.bfloat16)[None]
    frames = matmul(noisy_b, lat_w) + matmul(feats_b, time_w)
    words = matmul(words_in, text_w)
    hidden = jnp.concatenate([frames, words], 0)
    seq, width = hidden.shape
    heads = width // HD
    normed_b = layer_norm(hidden, gains[0]).astype(jnp.bfloat16)
    qkv = matmul(normed_b, qkv_w).astype(jnp.bfloat16)
    query = qkv[:frame_n, :width].reshape(frame_n, heads, HD)
    keys = qkv[:, width : 2 * width].reshape(seq, heads, HD)
    values = qkv[:, 2 * width :].reshape(seq, heads, HD)
    keep = (jnp.arange(seq) < frame_n) | (flag == 0)
    probs, lse_rows = attention_probs(query, keys, keep, None)
    mixed_b = (
        jnp.einsum(
            "hqk,khd->qhd", probs.astype(jnp.bfloat16), values, preferred_element_type=jnp.float32
        )
        .reshape(frame_n, width)
        .astype(jnp.bfloat16)
    )
    after = frames + matmul(mixed_b, out_w)
    normed2_b = layer_norm(after, gains[1]).astype(jnp.bfloat16)
    gate_up = matmul(normed2_b, gu_w).astype(jnp.bfloat16)
    ffw = gate_up.shape[1] // 2
    gate = gate_up[:, :ffw].astype(jnp.float32)
    up = gate_up[:, ffw:].astype(jnp.float32)
    inner_b = (jax.nn.silu(gate) * up).astype(jnp.bfloat16)
    final = after + matmul(inner_b, down_w)
    audio = final
    out_b = layer_norm(audio, gains[2]).astype(jnp.bfloat16)
    pred = matmul(out_b, lout_w)
    kept = (
        noisy_b,
        feats,
        hidden,
        normed_b,
        qkv,
        keep,
        lse_rows,
        mixed_b,
        after,
        normed2_b,
        gate_up,
        inner_b,
        audio,
        out_b,
    )
    return (pred, kept, words, audio)


def layer_backward(weights, kept, words_in, d_pred, d_audio_extra, d_words_extra):
    lat_w, time_w, text_w, qkv_w, out_w, gu_w, down_w, lout_w, gains = weights
    gains = gains.astype(jnp.float32)
    (
        noisy_b,
        feats,
        hidden,
        normed_b,
        qkv,
        keep,
        lse_rows,
        mixed_b,
        after,
        normed2_b,
        gate_up,
        inner_b,
        audio,
        out_b,
    ) = kept
    frame_n = audio.shape[0]
    seq, width = hidden.shape
    heads = width // HD
    d_pred_b = d_pred.astype(jnp.bfloat16)
    g_lout = matmul_tn(out_b, d_pred_b)
    d_audio, g_gain2 = norm_back(audio, gains[2], matmul_nt(d_pred_b, lout_w))
    d_final = d_audio + d_audio_extra
    d_final_b = d_final.astype(jnp.bfloat16)
    g_down = matmul_tn(inner_b, d_final_b)
    d_inner = matmul_nt(d_final_b, down_w)
    ffw = gate_up.shape[1] // 2
    gate = gate_up[:, :ffw].astype(jnp.float32)
    up = gate_up[:, ffw:].astype(jnp.float32)
    sig = jax.nn.sigmoid(gate)
    d_gate = d_inner * up * (sig * (1.0 + gate * (1.0 - sig)))
    d_up = d_inner * (gate * sig)
    d_gu_b = jnp.concatenate([d_gate, d_up], 1).astype(jnp.bfloat16)
    g_gu = matmul_tn(normed2_b, d_gu_b)
    d_after_n, g_gain1 = norm_back(after, gains[1], matmul_nt(d_gu_b, gu_w))
    d_after = d_final + d_after_n
    d_after_b = d_after.astype(jnp.bfloat16)
    g_outw = matmul_tn(mixed_b, d_after_b)
    d_mixed_b = matmul_nt(d_after_b, out_w).astype(jnp.bfloat16)
    d_mixed_b = d_mixed_b.reshape(frame_n, heads, HD)
    query = qkv[:frame_n, :width].reshape(frame_n, heads, HD)
    keys = qkv[:, width : 2 * width].reshape(seq, heads, HD)
    values = qkv[:, 2 * width :].reshape(seq, heads, HD)
    probs, _ = attention_probs(query, keys, keep, lse_rows)
    d_probs = jnp.einsum("qhd,khd->hqk", d_mixed_b, values, preferred_element_type=jnp.float32)
    d_values = jnp.einsum(
        "hqk,qhd->khd", probs.astype(jnp.bfloat16), d_mixed_b, preferred_element_type=jnp.float32
    )
    d_scores_b = (probs * (d_probs - jnp.sum(probs * d_probs, axis=-1, keepdims=True))).astype(
        jnp.bfloat16
    )
    d_query = jnp.einsum(
        "hqk,khd->qhd", d_scores_b, keys, preferred_element_type=jnp.float32
    ) * HD ** (-0.5)
    d_keys = jnp.einsum(
        "hqk,qhd->khd", d_scores_b, query, preferred_element_type=jnp.float32
    ) * HD ** (-0.5)
    d_qkv_b = jnp.concatenate(
        [
            jnp.pad(d_query.reshape(frame_n, width), ((0, seq - frame_n), (0, 0))),
            d_keys.reshape(seq, width),
            d_values.reshape(seq, width),
        ],
        1,
    ).astype(jnp.bfloat16)
    g_qkv = matmul_tn(normed_b, d_qkv_b)
    d_hidden_n, g_gain0 = norm_back(hidden, gains[0], matmul_nt(d_qkv_b, qkv_w))
    d_frames_b = (d_after + d_hidden_n[:frame_n]).astype(jnp.bfloat16)
    d_words_b = (d_hidden_n[frame_n:] + d_words_extra).astype(jnp.bfloat16)
    g_lat = matmul_tn(noisy_b, d_frames_b)
    column = jnp.sum(d_frames_b.astype(jnp.float32), 0)
    feats_low = feats.astype(jnp.bfloat16).astype(jnp.float32)
    g_time = feats_low[:, None] * column[None, :]
    g_text = matmul_tn(words_in, d_words_b)
    g_gains = jnp.stack([g_gain0, g_gain1, g_gain2])
    return (g_lat, g_time, g_text, g_qkv, g_outw, g_gu, g_down, g_lout, g_gains)


def links(sizes):
    steps = []
    for axis, size in (("fsdp", sizes[1]), ("dp", sizes[0])):
        bit = 1
        while bit < size:
            steps.append((axis, bit))
            bit *= 2
    return steps


def mine(axis, bit):
    return lax.rem(lax.axis_index(axis) // bit, 2)


def partner(axis, bit):
    return {axis: lax.axis_index(axis) + bit * (1 - 2 * mine(axis, bit))}


def greet(steps):
    barrier = pltpu.get_barrier_semaphore()
    for axis, bit in steps:
        pl.semaphore_signal(barrier, inc=1, device_id=partner(axis, bit), device_id_type=MESH)
    pl.semaphore_wait(barrier, len(steps))


def gather_kernel(sizes, block_ref, all_ref, send_sem, recv_sem):
    steps = links(sizes)
    me = lax.axis_index("dp") * sizes[1] + lax.axis_index("fsdp")
    greet(steps)
    all_ref[pl.ds(me, 1)] = block_ref[...][None]
    span = 1
    for index, (axis, bit) in enumerate(steps):
        held = all_ref.at[pl.ds((me // span) * span, span)]
        copy = pltpu.make_async_remote_copy(
            src_ref=held,
            dst_ref=held,
            send_sem=send_sem.at[index],
            recv_sem=recv_sem.at[index],
            device_id=partner(axis, bit),
            device_id_type=MESH,
        )
        copy.start()
        copy.wait()
        span *= 2


def gather_everywhere(block, sizes):
    count = len(links(sizes))
    return pl.pallas_call(
        functools.partial(gather_kernel, sizes),
        out_shape=jax.ShapeDtypeStruct((sizes[0] * sizes[1],) + block.shape, block.dtype),
        in_specs=[pl.BlockSpec(memory_space=pltpu.VMEM)],
        out_specs=pl.BlockSpec(memory_space=pltpu.VMEM),
        scratch_shapes=[pltpu.SemaphoreType.DMA((count,)), pltpu.SemaphoreType.DMA((count,))],
        compiler_params=pltpu.CompilerParams(collective_id=0, has_side_effects=True),
    )(block)


def sum_kernel(sizes, block_ref, sum_ref, part, came, send_sem, recv_sem):
    steps = links(sizes)
    greet(steps)
    part[0] = block_ref[...]
    for index, (axis, bit) in enumerate(steps):
        copy = pltpu.make_async_remote_copy(
            src_ref=part.at[index],
            dst_ref=came.at[index],
            send_sem=send_sem.at[index],
            recv_sem=recv_sem.at[index],
            device_id=partner(axis, bit),
            device_id_type=MESH,
        )
        copy.start()
        copy.wait()
        part[index + 1] = part[index] + came[index]
    sum_ref[...] = part[len(steps)]


def sum_everywhere(block, sizes):
    count = len(links(sizes))
    return pl.pallas_call(
        functools.partial(sum_kernel, sizes),
        out_shape=jax.ShapeDtypeStruct(block.shape, block.dtype),
        in_specs=[pl.BlockSpec(memory_space=pltpu.VMEM)],
        out_specs=pl.BlockSpec(memory_space=pltpu.VMEM),
        scratch_shapes=[
            pltpu.VMEM((count + 1,) + block.shape, block.dtype),
            pltpu.VMEM((count,) + block.shape, block.dtype),
            pltpu.SemaphoreType.DMA((count,)),
            pltpu.SemaphoreType.DMA((count,)),
        ],
        compiler_params=pltpu.CompilerParams(collective_id=1, has_side_effects=True),
    )(block)


def fold(share, rows):
    return share.reshape(rows, share.size // rows)


def gather_weights(masters):
    lat, time, text, qkv, out, gu, down, lout, gains = [w.astype(jnp.bfloat16) for w in masters]
    rows = qkv.shape[0]
    gains_t = jnp.pad(gains.T, ((0, 0), (0, LANES - gains.shape[0])))
    pieces = [qkv, out, fold(text, rows), fold(time, rows), lat.T, lout, gains_t]
    packed = jnp.concatenate(pieces, 1)
    gathered = lax.all_gather(packed, AXES, axis=0, tiled=True)
    full, start = [], 0
    for piece in pieces:
        full.append(gathered[:, start : start + piece.shape[1]])
        start += piece.shape[1]
    width = out.shape[1]
    return (
        full[4].T,
        full[3].reshape(-1, width),
        full[2].reshape(-1, width),
        full[0],
        full[1],
        lax.all_gather(gu, AXES, axis=0, tiled=True),
        lax.all_gather(down, AXES, axis=0, tiled=True),
        full[5],
        full[6][:, : gains.shape[0]].T,
    )


def scatter_grads(grads, masters):
    lat, time, text, qkv, out, gu, down, lout, gains = grads
    rows = qkv.shape[0]
    gains_t = jnp.pad(gains.T, ((0, 0), (0, LANES - gains.shape[0])))
    pieces = [fold(text, rows), fold(time, rows), lat.T, lout, gains_t]
    packed = jnp.concatenate(pieces, 1)

    def own(grad):
        return lax.psum_scatter(grad, AXES, scatter_dimension=0, tiled=True)

    summed = own(packed)
    parts, start = [], 0
    for piece in pieces:
        parts.append(summed[:, start : start + piece.shape[1]])
        start += piece.shape[1]
    return (
        parts[2].T,
        parts[1].reshape(masters[1].shape),
        parts[0].reshape(masters[2].shape),
        own(qkv),
        own(out),
        own(gu),
        own(down),
        parts[3],
        parts[4][:, : gains.shape[0]].T,
    )


def contrast(audio_vec, text_vec, empty, negatives, sizes):
    width = audio_vec.shape[0]
    lines = width // LANES
    me = lax.axis_index(AXES)
    facts = jnp.concatenate([empty, me[None], negatives[0]]).astype(jnp.float32)
    block = jnp.concatenate(
        [
            audio_vec.reshape(lines, LANES),
            text_vec.astype(jnp.bfloat16).astype(jnp.float32).reshape(lines, LANES),
            jnp.pad(facts, (0, LANES - facts.shape[0]))[None],
        ]
    )
    block = jnp.pad(block, ((0, -block.shape[0] % 8), (0, 0)))
    everyone = gather_everywhere(block, sizes)
    clips = everyone.shape[0]
    audios = everyone[:, :lines].reshape(clips, width)
    texts = everyone[:, lines : 2 * lines].reshape(clips, width)
    flags = everyone[:, 2 * lines, 0]
    picks = everyone[:, 2 * lines, 1 : 2 + negatives.shape[1]].astype(jnp.int32)
    coeff = INV_TEMP / width
    places = jnp.arange(clips, dtype=jnp.int32)
    onehot = (picks[:, :, None] == places[None, None, :]).astype(jnp.float32)
    cross = coeff * jnp.einsum("cd,td->ct", audios, texts, precision=HIGH)
    sims = jnp.sum(onehot * cross[:, None, :], axis=2)
    total = jax.nn.logsumexp(sims, axis=1, keepdims=True)
    weights = CON_WEIGHT * (1.0 - flags)[:, None]
    first_pick = (jnp.arange(sims.shape[1]) == 0).astype(jnp.float32)[None, :]
    d_sims = weights * (jnp.exp(sims - total) - first_pick)
    d_cross = coeff * jnp.sum(onehot * d_sims[:, :, None], axis=1)
    is_me = (places == me).astype(jnp.float32)
    d_audio_vec = jnp.dot(jnp.sum(d_cross * is_me[:, None], axis=0), texts, precision=HIGH)
    d_text_vec = jnp.dot(jnp.sum(d_cross * is_me[None, :], axis=1), audios, precision=HIGH)
    con = jnp.sum((total[:, 0] - sims[:, 0]) * is_me)
    return (d_audio_vec, d_text_vec, con)


def body(
    sizes,
    latent,
    noise,
    text,
    steps,
    empty,
    negatives,
    latent_in,
    time_proj,
    text_proj,
    attn_qkv,
    attn_out,
    glu_in,
    glu_out,
    latent_out,
    norm_gains,
    first_latent_in,
    first_time_proj,
    first_text_proj,
    first_attn_qkv,
    first_attn_out,
    first_glu_in,
    first_glu_out,
    first_latent_out,
    first_norm_gains,
    second_latent_in,
    second_time_proj,
    second_text_proj,
    second_attn_qkv,
    second_attn_out,
    second_glu_in,
    second_glu_out,
    second_latent_out,
    second_norm_gains,
):
    masters = (
        latent_in,
        time_proj,
        text_proj,
        attn_qkv,
        attn_out,
        glu_in,
        glu_out,
        latent_out,
        norm_gains,
    )
    firsts = (
        first_latent_in,
        first_time_proj,
        first_text_proj,
        first_attn_qkv,
        first_attn_out,
        first_glu_in,
        first_glu_out,
        first_latent_out,
        first_norm_gains,
    )
    seconds = (
        second_latent_in,
        second_time_proj,
        second_text_proj,
        second_attn_qkv,
        second_attn_out,
        second_glu_in,
        second_glu_out,
        second_latent_out,
        second_norm_gains,
    )
    weights = gather_weights(masters)
    step_id = steps[0]
    flag = empty[0]
    place = (step_id.astype(jnp.float32) + 0.5) / NB
    alpha = jnp.cos(0.5 * jnp.pi * place)
    sigma = jnp.sin(0.5 * jnp.pi * place)
    clean = latent[0]
    fresh = noise[0]
    noisy = alpha * clean + sigma * fresh
    target = alpha * fresh - sigma * clean
    feats = time_features(step_id)
    words_in = text[0]
    pred, kept, words, audio = layer_forward(weights, noisy, feats, words_in, flag)
    error = pred - target
    frame_n, chans = pred.shape
    mse = jnp.sum(error * error) / (frame_n * chans)
    d_pred = 2.0 * error / (frame_n * chans)
    audio_vec, pull_audio = jax.vjp(unit_scale, jnp.mean(audio, 0))
    text_vec, pull_text = jax.vjp(unit_scale, jnp.mean(words, 0))
    d_audio_vec, d_text_vec, con = contrast(audio_vec, text_vec, empty, negatives, sizes)
    weight = CON_WEIGHT * (1 - flag).astype(jnp.float32)
    d_audio_extra = pull_audio(d_audio_vec)[0][None, :] / frame_n
    d_words_extra = pull_text(d_text_vec)[0][None, :] / words.shape[0]
    grads = layer_backward(weights, kept, words_in, d_pred, d_audio_extra, d_words_extra)
    shares = scatter_grads(grads, masters)
    squares = jnp.zeros((), jnp.float32)
    for share in shares:
        squares = squares + jnp.sum(share * share)
    loss_local = mse + weight * con
    bucket_local = (jnp.arange(NB, dtype=jnp.int32) == step_id).astype(jnp.float32) * mse
    line = jnp.concatenate([loss_local[None], squares[None], bucket_local])
    line = jnp.pad(line, (0, LANES - line.shape[0]))[None]
    sums = sum_everywhere(jnp.pad(line, ((0, 7), (0, 0))), sizes)[0]
    loss_sum, total_sq, bucket_sums = sums[0], sums[1], sums[2 : 2 + NB]
    grad_norm = jnp.sqrt(total_sq)
    scale = jnp.minimum(1.0, CLIP_NORM / (grad_norm + 1e-06))
    new_weights, new_firsts, new_seconds = ([], [], [])
    for index, (master, first, second, share) in enumerate(zip(masters, firsts, seconds, shares)):
        rate = GAIN_RATE if index == len(masters) - 1 else RATE
        grad = share * scale
        first = BETA_ONE * first + (1.0 - BETA_ONE) * grad
        second = BETA_TWO * second + (1.0 - BETA_TWO) * grad * grad
        fixed_first = first / (1.0 - BETA_ONE**STEP)
        fixed_second = second / (1.0 - BETA_TWO**STEP)
        master = master - rate * (
            fixed_first / (jnp.sqrt(fixed_second) + ADAM_EPS) + DECAY * master
        )
        new_weights.append(master)
        new_firsts.append(first)
        new_seconds.append(second)
    return (
        loss_sum,
        bucket_sums,
        grad_norm,
        new_weights[0],
        new_weights[1],
        new_weights[2],
        new_weights[3],
        new_weights[4],
        new_weights[5],
        new_weights[6],
        new_weights[7],
        new_weights[8],
        new_firsts[0],
        new_firsts[1],
        new_firsts[2],
        new_firsts[3],
        new_firsts[4],
        new_firsts[5],
        new_firsts[6],
        new_firsts[7],
        new_firsts[8],
        new_seconds[0],
        new_seconds[1],
        new_seconds[2],
        new_seconds[3],
        new_seconds[4],
        new_seconds[5],
        new_seconds[6],
        new_seconds[7],
        new_seconds[8],
    )


def solution(mesh):
    sizes = (mesh.shape["dp"], mesh.shape["fsdp"])
    return jax.shard_map(
        functools.partial(body, sizes),
        mesh=mesh,
        in_specs=(
            P(("dp", "fsdp"), None, None),
            P(("dp", "fsdp"), None, None),
            P(("dp", "fsdp"), None, None),
            P(("dp", "fsdp")),
            P(("dp", "fsdp")),
            P(("dp", "fsdp"), None),
            P(None, ("dp", "fsdp")),
            P(("dp", "fsdp"), None),
            P(("dp", "fsdp"), None),
            P(("dp", "fsdp"), None),
            P(("dp", "fsdp"), None),
            P(("dp", "fsdp"), None),
            P(("dp", "fsdp"), None),
            P(("dp", "fsdp"), None),
            P(None, ("dp", "fsdp")),
            P(None, ("dp", "fsdp")),
            P(("dp", "fsdp"), None),
            P(("dp", "fsdp"), None),
            P(("dp", "fsdp"), None),
            P(("dp", "fsdp"), None),
            P(("dp", "fsdp"), None),
            P(("dp", "fsdp"), None),
            P(("dp", "fsdp"), None),
            P(None, ("dp", "fsdp")),
            P(None, ("dp", "fsdp")),
            P(("dp", "fsdp"), None),
            P(("dp", "fsdp"), None),
            P(("dp", "fsdp"), None),
            P(("dp", "fsdp"), None),
            P(("dp", "fsdp"), None),
            P(("dp", "fsdp"), None),
            P(("dp", "fsdp"), None),
            P(None, ("dp", "fsdp")),
        ),
        out_specs=(
            P(),
            P(),
            P(),
            P(None, ("dp", "fsdp")),
            P(("dp", "fsdp"), None),
            P(("dp", "fsdp"), None),
            P(("dp", "fsdp"), None),
            P(("dp", "fsdp"), None),
            P(("dp", "fsdp"), None),
            P(("dp", "fsdp"), None),
            P(("dp", "fsdp"), None),
            P(None, ("dp", "fsdp")),
            P(None, ("dp", "fsdp")),
            P(("dp", "fsdp"), None),
            P(("dp", "fsdp"), None),
            P(("dp", "fsdp"), None),
            P(("dp", "fsdp"), None),
            P(("dp", "fsdp"), None),
            P(("dp", "fsdp"), None),
            P(("dp", "fsdp"), None),
            P(None, ("dp", "fsdp")),
            P(None, ("dp", "fsdp")),
            P(("dp", "fsdp"), None),
            P(("dp", "fsdp"), None),
            P(("dp", "fsdp"), None),
            P(("dp", "fsdp"), None),
            P(("dp", "fsdp"), None),
            P(("dp", "fsdp"), None),
            P(("dp", "fsdp"), None),
            P(None, ("dp", "fsdp")),
        ),
        check_vma=False,
    )
```

```python
import functools
import math

import jax
import jax.numpy as jnp
from jax import lax
from jax.experimental import pallas as pl
from jax.experimental.pallas import tpu as pltpu
from jax.sharding import PartitionSpec as P

AXES = ("dp", "fsdp")
MESH = pl.DeviceIdType.MESH
LANES = 128
COLS = 256
LAG = 2
SLOTS = 2 * LAG

HD = 64
TF = 256
NB = 8
STEP = 10


EPS_NORM = 1e-05
BETA_ONE = 0.9
BETA_TWO = 0.95
ADAM_EPS = 1e-08
RATE = 0.02
GAIN_RATE = 0.3
DECAY = 0.01
CLIP_NORM = 0.05
CON_WEIGHT = 0.5
INV_TEMP = 50.0
HIGH = lax.Precision.HIGHEST


def matmul(left, right):
    return jnp.dot(left, right, preferred_element_type=jnp.float32)


def matmul_tn(left, right):
    return lax.dot_general(
        left, right, (((0,), (0,)), ((), ())), preferred_element_type=jnp.float32
    )


def matmul_nt(left, right):
    return lax.dot_general(
        left, right, (((1,), (1,)), ((), ())), preferred_element_type=jnp.float32
    )


def layer_norm(x, gain):
    cent = x - jnp.mean(x, axis=-1, keepdims=True)
    var = jnp.mean(cent * cent, axis=-1, keepdims=True)
    return cent * lax.rsqrt(var + EPS_NORM) * gain


def norm_back(x, gain, grad):
    _, pull = jax.vjp(layer_norm, x, gain)
    return pull(grad)


def unit_scale(x):
    return x * lax.rsqrt(jnp.mean(x * x) + EPS_NORM)


def time_features(step_id):
    place = (step_id.astype(jnp.float32) + 0.5) / NB
    half = TF // 2
    freqs = jnp.exp(jnp.arange(half, dtype=jnp.float32) * (math.log(100.0) / half))
    angle = place * freqs
    return jnp.concatenate([jnp.cos(angle), jnp.sin(angle)])


def attention_probs(query, keys, keep, lse_rows):
    scores = jnp.einsum("qhd,khd->hqk", query, keys, preferred_element_type=jnp.float32) * HD ** (
        -0.5
    )
    scores = jnp.where(keep[None, None, :], scores, -1e30)
    if lse_rows is None:
        top = jnp.max(scores, axis=-1, keepdims=True)
        lse_rows = top + jnp.log(jnp.sum(jnp.exp(scores - top), axis=-1, keepdims=True))
    return (jnp.exp(scores - lse_rows), lse_rows)


def layer_forward(weights, noisy, feats, words_in, flag):
    lat_w, time_w, text_w, qkv_w, out_w, gu_w, down_w, lout_w, gains = weights
    gains = gains.astype(jnp.float32)
    frame_n = noisy.shape[0]
    noisy_b = noisy.astype(jnp.bfloat16)
    feats_b = feats.astype(jnp.bfloat16)[None]
    frames = matmul(noisy_b, lat_w) + matmul(feats_b, time_w)
    words = matmul(words_in, text_w)
    hidden = jnp.concatenate([frames, words], 0)
    seq, width = hidden.shape
    heads = width // HD
    normed_b = layer_norm(hidden, gains[0]).astype(jnp.bfloat16)
    qkv = matmul(normed_b, qkv_w).astype(jnp.bfloat16)
    query = qkv[:frame_n, :width].reshape(frame_n, heads, HD)
    keys = qkv[:, width : 2 * width].reshape(seq, heads, HD)
    values = qkv[:, 2 * width :].reshape(seq, heads, HD)
    keep = (jnp.arange(seq) < frame_n) | (flag == 0)
    probs, lse_rows = attention_probs(query, keys, keep, None)
    mixed_b = (
        jnp.einsum(
            "hqk,khd->qhd", probs.astype(jnp.bfloat16), values, preferred_element_type=jnp.float32
        )
        .reshape(frame_n, width)
        .astype(jnp.bfloat16)
    )
    after = frames + matmul(mixed_b, out_w)
    normed2_b = layer_norm(after, gains[1]).astype(jnp.bfloat16)
    gate_up = matmul(normed2_b, gu_w).astype(jnp.bfloat16)
    ffw = gate_up.shape[1] // 2
    gate = gate_up[:, :ffw].astype(jnp.float32)
    up = gate_up[:, ffw:].astype(jnp.float32)
    inner_b = (jax.nn.silu(gate) * up).astype(jnp.bfloat16)
    final = after + matmul(inner_b, down_w)
    audio = final
    out_b = layer_norm(audio, gains[2]).astype(jnp.bfloat16)
    pred = matmul(out_b, lout_w)
    kept = (
        noisy_b,
        feats,
        hidden,
        normed_b,
        qkv,
        keep,
        lse_rows,
        mixed_b,
        after,
        normed2_b,
        gate_up,
        inner_b,
        audio,
        out_b,
    )
    return (pred, kept, words, audio)


def layer_backward(weights, kept, words_in, d_pred, d_audio_extra, d_words_extra):
    lat_w, time_w, text_w, qkv_w, out_w, gu_w, down_w, lout_w, gains = weights
    gains = gains.astype(jnp.float32)
    (
        noisy_b,
        feats,
        hidden,
        normed_b,
        qkv,
        keep,
        lse_rows,
        mixed_b,
        after,
        normed2_b,
        gate_up,
        inner_b,
        audio,
        out_b,
    ) = kept
    frame_n = audio.shape[0]
    seq, width = hidden.shape
    heads = width // HD
    d_pred_b = d_pred.astype(jnp.bfloat16)
    g_lout = matmul_tn(out_b, d_pred_b)
    d_audio, g_gain2 = norm_back(audio, gains[2], matmul_nt(d_pred_b, lout_w))
    d_final = d_audio + d_audio_extra
    d_final_b = d_final.astype(jnp.bfloat16)
    d_inner = matmul_nt(d_final_b, down_w)
    ffw = gate_up.shape[1] // 2
    gate = gate_up[:, :ffw].astype(jnp.float32)
    up = gate_up[:, ffw:].astype(jnp.float32)
    sig = jax.nn.sigmoid(gate)
    d_gate = d_inner * up * (sig * (1.0 + gate * (1.0 - sig)))
    d_up = d_inner * (gate * sig)
    d_gu_b = jnp.concatenate([d_gate, d_up], 1).astype(jnp.bfloat16)
    d_after_n, g_gain1 = norm_back(after, gains[1], matmul_nt(d_gu_b, gu_w))
    d_after = d_final + d_after_n
    d_after_b = d_after.astype(jnp.bfloat16)
    d_mixed_b = matmul_nt(d_after_b, out_w).astype(jnp.bfloat16)
    d_mixed_b = d_mixed_b.reshape(frame_n, heads, HD)
    query = qkv[:frame_n, :width].reshape(frame_n, heads, HD)
    keys = qkv[:, width : 2 * width].reshape(seq, heads, HD)
    values = qkv[:, 2 * width :].reshape(seq, heads, HD)
    probs, _ = attention_probs(query, keys, keep, lse_rows)
    d_probs = jnp.einsum("qhd,khd->hqk", d_mixed_b, values, preferred_element_type=jnp.float32)
    d_values = jnp.einsum(
        "hqk,qhd->khd", probs.astype(jnp.bfloat16), d_mixed_b, preferred_element_type=jnp.float32
    )
    d_scores_b = (probs * (d_probs - jnp.sum(probs * d_probs, axis=-1, keepdims=True))).astype(
        jnp.bfloat16
    )
    d_query = jnp.einsum(
        "hqk,khd->qhd", d_scores_b, keys, preferred_element_type=jnp.float32
    ) * HD ** (-0.5)
    d_keys = jnp.einsum(
        "hqk,qhd->khd", d_scores_b, query, preferred_element_type=jnp.float32
    ) * HD ** (-0.5)
    d_qkv_b = jnp.concatenate(
        [
            jnp.pad(d_query.reshape(frame_n, width), ((0, seq - frame_n), (0, 0))),
            d_keys.reshape(seq, width),
            d_values.reshape(seq, width),
        ],
        1,
    ).astype(jnp.bfloat16)
    d_hidden_n, g_gain0 = norm_back(hidden, gains[0], matmul_nt(d_qkv_b, qkv_w))
    d_frames_b = (d_after + d_hidden_n[:frame_n]).astype(jnp.bfloat16)
    d_words_b = (d_hidden_n[frame_n:] + d_words_extra).astype(jnp.bfloat16)
    g_lat = matmul_tn(noisy_b, d_frames_b)
    column = jnp.sum(d_frames_b.astype(jnp.float32), 0)
    feats_low = lax.reduce_precision(feats, 8, 7)
    g_time = feats_low[:, None] * column[None, :]
    g_text = matmul_tn(words_in, d_words_b)
    g_gains = jnp.stack([g_gain0, g_gain1, g_gain2])
    pairs = (
        (normed2_b, d_gu_b),
        (inner_b, d_final_b),
        (mixed_b, d_after_b),
        (normed_b, d_qkv_b),
    )
    return (pairs, (g_lat, g_time, g_text, g_lout, g_gains))


def links(sizes):
    steps = []
    for axis, size in (("fsdp", sizes[1]), ("dp", sizes[0])):
        bit = 1
        while bit < size:
            steps.append((axis, bit))
            bit *= 2
    return steps


def mine(axis, bit):
    return lax.rem(lax.axis_index(axis) // bit, 2)


def partner(axis, bit):
    return {axis: lax.axis_index(axis) + bit * (1 - 2 * mine(axis, bit))}


def greet(steps):
    barrier = pltpu.get_barrier_semaphore()
    for axis, bit in steps:
        pl.semaphore_signal(barrier, inc=1, device_id=partner(axis, bit), device_id_type=MESH)
    pl.semaphore_wait(barrier, len(steps))


def gather_kernel(sizes, block_ref, all_ref, send_sem, recv_sem):
    steps = links(sizes)
    me = lax.axis_index("dp") * sizes[1] + lax.axis_index("fsdp")
    greet(steps)
    all_ref[pl.ds(me, 1)] = block_ref[...][None]
    span = 1
    for index, (axis, bit) in enumerate(steps):
        held = all_ref.at[pl.ds((me // span) * span, span)]
        copy = pltpu.make_async_remote_copy(
            src_ref=held,
            dst_ref=held,
            send_sem=send_sem.at[index],
            recv_sem=recv_sem.at[index],
            device_id=partner(axis, bit),
            device_id_type=MESH,
        )
        copy.start()
        copy.wait()
        span *= 2


def gather_everywhere(block, sizes):
    count = len(links(sizes))
    return pl.pallas_call(
        functools.partial(gather_kernel, sizes),
        out_shape=jax.ShapeDtypeStruct((sizes[0] * sizes[1],) + block.shape, block.dtype),
        in_specs=[pl.BlockSpec(memory_space=pltpu.VMEM)],
        out_specs=pl.BlockSpec(memory_space=pltpu.VMEM),
        scratch_shapes=[pltpu.SemaphoreType.DMA((count,)), pltpu.SemaphoreType.DMA((count,))],
        compiler_params=pltpu.CompilerParams(collective_id=0, has_side_effects=True),
    )(block)


def sum_kernel(sizes, block_ref, sum_ref, part, came, send_sem, recv_sem):
    steps = links(sizes)
    greet(steps)
    part[0] = block_ref[...]
    for index, (axis, bit) in enumerate(steps):
        copy = pltpu.make_async_remote_copy(
            src_ref=part.at[index],
            dst_ref=came.at[index],
            send_sem=send_sem.at[index],
            recv_sem=recv_sem.at[index],
            device_id=partner(axis, bit),
            device_id_type=MESH,
        )
        copy.start()
        copy.wait()
        part[index + 1] = part[index] + came[index]
    sum_ref[...] = part[len(steps)]


def sum_everywhere(block, sizes):
    count = len(links(sizes))
    return pl.pallas_call(
        functools.partial(sum_kernel, sizes),
        out_shape=jax.ShapeDtypeStruct(block.shape, block.dtype),
        in_specs=[pl.BlockSpec(memory_space=pltpu.VMEM)],
        out_specs=pl.BlockSpec(memory_space=pltpu.VMEM),
        scratch_shapes=[
            pltpu.VMEM((count + 1,) + block.shape, block.dtype),
            pltpu.VMEM((count,) + block.shape, block.dtype),
            pltpu.SemaphoreType.DMA((count,)),
            pltpu.SemaphoreType.DMA((count,)),
        ],
        compiler_params=pltpu.CompilerParams(collective_id=1, has_side_effects=True),
    )(block)


def scatter_kernel(plan, *refs):
    rows = plan["rows"]
    (xt_gu, xt_down, xt_out, xt_qkv, dy_gu, dy_down, dy_out, dy_qkv, misc, *rest) = refs
    (o_gu, o_down, o_out, o_qkv, o_misc, *rest) = rest
    (xs, xq, dya, dyq, ss, rr, kk, final, load_sem, dy_sem, misc_sem, send_sem, recv_sem, out_sem) = rest
    n_gu, n_down, n_out, n_qkv, n_misc = plan["tiles"]
    folds = plan["folds"]
    e_gu = n_gu
    e_down = e_gu + n_down
    e_out = e_down + n_out
    e_qkv = e_out + n_qkv
    total = e_qkv + n_misc
    per_fold = n_down // folds
    stages = (("dp", 1), ("dp", 2), ("fsdp", 1), ("fsdp", 2), ("fsdp", 4))
    greet(stages)

    dp, fsdp = lax.axis_index("dp"), lax.axis_index("fsdp")
    core, x = lax.rem(dp, 2), dp // 2
    y, z0, z1 = lax.rem(fsdp, 2), lax.rem(fsdp // 2, 2), fsdp // 4

    def owner(block):
        def bit(mine, weight):
            same = lax.rem(block // weight, 2)
            return mine + (1 - same) * (1 - 2 * mine)

        where = bit(x, 8) * 2 + bit(core, 16)
        return where * 8 + bit(z1, 1) * 4 + bit(z0, 2) * 2 + bit(y, 4)

    def load(source, fold, dest, index, reach):
        def one(block, carry):
            first = pl.multiple_of(owner(block) * (reach * rows) + fold * rows, 16)
            pltpu.make_async_copy(
                source.at[pl.ds(first, rows)], dest.at[block], load_sem.at[index]
            ).start()
            return carry

        lax.fori_loop(0, 32, one, 0)

    load(xt_gu, 0, xs.at[0], 0, 1)
    for fold in range(folds):
        load(xt_down, fold, xs.at[1 + fold], 1 + fold, folds)
    load(xt_out, 0, xs.at[1 + folds], 1 + folds, 1)
    load(xt_qkv, 0, xq, 2 + folds, 1)

    def columns(tile):
        return pl.ds(pl.multiple_of(tile * COLS, COLS), COLS)

    def fetch(tile):
        slot = lax.rem(tile, 2)
        for low, high, source, dest, start, wrap in (
            (0, e_gu, dy_gu, dya, 0, n_gu),
            (e_gu, e_down, dy_down, dya, e_gu, per_fold),
            (e_down, e_out, dy_out, dya, e_down, n_out),
            (e_out, e_qkv, dy_qkv, dyq, e_out, n_qkv),
        ):

            @pl.when((tile >= low) & (tile < high))
            def _(source=source, dest=dest, start=start, wrap=wrap):
                pltpu.make_async_copy(
                    source.at[:, columns(lax.rem(tile - start, wrap))], dest.at[slot], dy_sem.at[slot]
                ).start()

    def product(left, right, half, keep):
        def part(step, carry):
            some = pl.ds(pl.multiple_of(step * 4, 4), 4)
            lhs = left[pl.ds(half * 16 + step * 4, 4)]
            out = jnp.dot(
                lhs.reshape(4 * rows, lhs.shape[-1]), right[...], preferred_element_type=jnp.float32
            )
            keep[some] = out.reshape(4, rows, COLS)
            return carry

        lax.fori_loop(0, 4, part, 0)

    def copy(stage, parity, tile):
        axis, bit = stages[stage]
        if parity and stage in (1, 2):
            axis, bit = stages[3 - stage]
        slot = lax.rem(tile, SLOTS)
        return pltpu.make_async_remote_copy(
            src_ref=ss[stage].at[slot],
            dst_ref=rr[stage].at[slot],
            send_sem=send_sem.at[stage, slot],
            recv_sem=recv_sem.at[stage, slot],
            device_id=partner(axis, bit),
            device_id_type=MESH,
        )

    def out_copies(tile):
        slot = lax.rem(tile, 2)
        for low, high, dest, fold_size in (
            (0, e_gu, o_gu, n_gu),
            (e_gu, e_down, o_down, per_fold),
            (e_down, e_out, o_out, n_out),
            (e_out, e_qkv, o_qkv, n_qkv),
            (e_qkv, total, o_misc, n_misc),
        ):

            @pl.when((tile >= low) & (tile < high))
            def _(low=low, dest=dest, fold_size=fold_size):
                fold = (tile - low) // fold_size
                first = pl.multiple_of(fold * rows, 8)
                pltpu.make_async_copy(
                    final.at[slot],
                    dest.at[pl.ds(first, rows), columns(lax.rem(tile - low, fold_size))],
                    out_sem.at[slot],
                ).start()

    def wait_out(tile):
        slot = lax.rem(tile, 2)
        pltpu.make_async_copy(final.at[slot], o_gu.at[:, columns(0)], out_sem.at[slot]).wait()

    def freed(stage, parity, tile):
        @pl.when((tile >= SLOTS) & (tile < total + SLOTS))
        def _():
            copy(stage, parity, tile - SLOTS).wait_send()

    def make(parity, tile):
        freed(0, parity, tile)

        @pl.when(tile < total)
        def _():
            slot = lax.rem(tile, SLOTS)
            send, keep = ss[0].at[slot], kk[0].at[parity]

            @pl.when(tile + 1 < e_qkv)
            def _():
                fetch(tile + 1)

            @pl.when(tile < e_out)
            def _():
                pltpu.make_async_copy(
                    dy_gu.at[:, columns(0)], dya.at[parity], dy_sem.at[parity]
                ).wait()
                which = (
                    jnp.where(tile >= e_gu, 1 + (tile - e_gu) // per_fold, 0)
                )
                left = xs.at[which]
                product(left, dya.at[parity], 0, send)
                copy(0, parity, tile).start()
                product(left, dya.at[parity], 1, keep)

            @pl.when((tile >= e_out) & (tile < e_qkv))
            def _():
                pltpu.make_async_copy(
                    dy_qkv.at[:, columns(0)], dyq.at[parity], dy_sem.at[parity]
                ).wait()
                product(xq, dyq.at[parity], 0, send)
                copy(0, parity, tile).start()
                product(xq, dyq.at[parity], 1, keep)

            @pl.when(tile >= e_qkv)
            def _():
                def one(block, carry):
                    def source(half):
                        first = pl.multiple_of(owner(block + 16 * half) * rows, 8)
                        return misc.at[pl.ds(first, rows), columns(tile - e_qkv)]

                    pltpu.make_async_copy(source(0), send.at[block], misc_sem.at[0]).start()
                    pltpu.make_async_copy(source(1), keep.at[block], misc_sem.at[1]).start()
                    return carry

                lax.fori_loop(0, 16, one, 0)
                pltpu.make_async_copy(send, send, misc_sem.at[0]).wait()
                copy(0, parity, tile).start()
                pltpu.make_async_copy(keep, keep, misc_sem.at[1]).wait()

    def pass_on(stage, parity, tile):
        freed(stage, parity, tile)

        @pl.when((tile >= 0) & (tile < total))
        def _():
            slot = lax.rem(tile + SLOTS, SLOTS)
            copy(stage - 1, parity, tile).wait_recv()
            came, held = rr[stage - 1].at[slot], kk[stage - 1].at[parity]
            send, keep = ss[stage].at[slot], kk[stage].at[parity]
            half = 32 >> (stage + 1)
            group = half // 2 if (stage == 1 and parity) else half

            def part(block, carry):
                low = block + (block // group) * group
                send[block] = (held[low] + came[low].astype(jnp.float32)).astype(send.dtype)
                return carry

            def rest(block, carry):
                high = block + (block // group) * group + group
                keep[block] = held[high] + came[high].astype(jnp.float32)
                return carry

            lax.fori_loop(0, half, part, 0)
            copy(stage, parity, tile).start()
            lax.fori_loop(0, half, rest, 0)

    def finish(parity, tile):
        @pl.when((tile >= 2) & (tile < total + 2))
        def _():
            wait_out(tile)

        @pl.when((tile >= 0) & (tile < total))
        def _():
            slot = lax.rem(tile + SLOTS, SLOTS)
            copy(4, parity, tile).wait_recv()
            final[parity] = kk[4][parity, 0] + rr[4][slot, 0].astype(jnp.float32)
            out_copies(tile)

    fetch(0)
    for index in range(3 + folds):
        dest = xq if index == 2 + folds else xs.at[index]
        pltpu.make_async_copy(dest, dest, load_sem.at[index]).wait()

    def pair(step, carry):
        for parity in range(2):
            now = step * 2 + parity
            finish(parity, now - 5 * LAG)
            for stage in (4, 3, 2, 1):
                pass_on(stage, parity, now - stage * LAG)
            make(parity, now)
        return carry

    lax.fori_loop(0, (total + 4 * LAG + SLOTS + 1) // 2, pair, 0)


def scatter_sums(xts, dys, misc):
    xt_gu, xt_down, xt_out, xt_qkv = xts
    dy_gu, dy_down, dy_out, dy_qkv = dys
    rows = xt_gu.shape[0] // 32
    folds = xt_down.shape[0] // xt_gu.shape[0]
    counts = [d.shape[1] // COLS for d in (dy_gu, dy_down, dy_out, dy_qkv, misc)]
    counts[1] *= folds
    plan = {"rows": rows, "tiles": tuple(counts), "folds": folds}
    sizes = [16 >> stage for stage in range(5)]
    f32, bf16 = jnp.float32, jnp.bfloat16
    link_types = (f32, bf16, bf16, f32, f32)
    scratch = [
        pltpu.VMEM((2 + folds, 32, rows, xt_gu.shape[1]), bf16),
        pltpu.VMEM((32, rows, xt_qkv.shape[1]), bf16),
        pltpu.VMEM((2, xt_gu.shape[1], COLS), bf16),
        pltpu.VMEM((2, xt_qkv.shape[1], COLS), bf16),
        [pltpu.VMEM((SLOTS, n, rows, COLS), t) for n, t in zip(sizes, link_types)],
        [pltpu.VMEM((SLOTS, n, rows, COLS), t) for n, t in zip(sizes, link_types)],
        [pltpu.VMEM((2, n, rows, COLS), f32) for n in sizes],
        pltpu.VMEM((2, rows, COLS), f32),
        pltpu.SemaphoreType.DMA((3 + folds,)),
        pltpu.SemaphoreType.DMA((2,)),
        pltpu.SemaphoreType.DMA((2,)),
        pltpu.SemaphoreType.DMA((5, SLOTS)),
        pltpu.SemaphoreType.DMA((5, SLOTS)),
        pltpu.SemaphoreType.DMA((2,)),
    ]
    outs = [
        jax.ShapeDtypeStruct((rows * n, d.shape[1]), f32)
        for d, n in ((dy_gu, 1), (dy_down, folds), (dy_out, 1), (dy_qkv, 1), (misc, 1))
    ]
    return pl.pallas_call(
        functools.partial(scatter_kernel, plan),
        out_shape=outs,
        in_specs=[pl.BlockSpec(memory_space=pl.ANY)] * 9,
        out_specs=[pl.BlockSpec(memory_space=pl.ANY)] * 5,
        scratch_shapes=scratch,
        compiler_params=pltpu.CompilerParams(
            collective_id=2, has_side_effects=True, vmem_limit_bytes=48 * 1024 * 1024
        ),
    )(*xts, *dys, misc)


def fold(share, rows):
    return share.reshape(rows, share.size // rows)


def gather_weights(masters):
    lat, time, text, qkv, out, gu, down, lout, gains = [w.astype(jnp.bfloat16) for w in masters]
    rows = qkv.shape[0]
    gains_t = jnp.pad(gains.T, ((0, 0), (0, LANES - gains.shape[0])))
    pieces = [qkv, out, fold(text, rows), fold(time, rows), lat.T, lout, gains_t]
    packed = jnp.concatenate(pieces, 1)
    gathered = lax.all_gather(packed, AXES, axis=0, tiled=True)
    full, start = [], 0
    for piece in pieces:
        full.append(gathered[:, start : start + piece.shape[1]])
        start += piece.shape[1]
    width = out.shape[1]
    return (
        full[4].T,
        full[3].reshape(-1, width),
        full[2].reshape(-1, width),
        full[0],
        full[1],
        lax.all_gather(gu, AXES, axis=0, tiled=True),
        lax.all_gather(down, AXES, axis=0, tiled=True),
        full[5],
        full[6][:, : gains.shape[0]].T,
    )


def scatter_grads(pairs, small, masters, sizes):
    lat, time, text, lout, gains = small
    rows = lout.shape[0]
    gains_t = jnp.pad(gains.T, ((0, 0), (0, LANES - gains.shape[0])))
    pieces = [fold(text, rows), fold(time, rows), lat.T, lout, gains_t]
    packed = jnp.concatenate(pieces, 1)
    if sizes == (4, 8) and rows % (32 * 16) == 0:
        gu, down, out, qkv, summed = scatter_sums([x.T for x, _ in pairs], [d for _, d in pairs], packed)
    else:
        grads = [matmul_tn(x, d) for x, d in pairs] + [packed]
        gu, down, out, qkv, summed = [
            lax.psum_scatter(g, AXES, scatter_dimension=0, tiled=True) for g in grads
        ]
    parts, start = [], 0
    for piece in pieces:
        parts.append(summed[:, start : start + piece.shape[1]])
        start += piece.shape[1]
    return (
        parts[2].T,
        parts[1].reshape(masters[1].shape),
        parts[0].reshape(masters[2].shape),
        qkv,
        out,
        gu,
        down,
        parts[3],
        parts[4][:, : gains.shape[0]].T,
    )


def contrast(audio_vec, text_vec, empty, negatives, sizes):
    width = audio_vec.shape[0]
    lines = width // LANES
    me = lax.axis_index(AXES)
    facts = jnp.concatenate([empty, me[None], negatives[0]]).astype(jnp.float32)
    block = jnp.concatenate(
        [
            audio_vec.reshape(lines, LANES),
            lax.reduce_precision(text_vec, 8, 7).reshape(lines, LANES),
            jnp.pad(facts, (0, LANES - facts.shape[0]))[None],
        ]
    )
    block = jnp.pad(block, ((0, -block.shape[0] % 8), (0, 0)))
    everyone = gather_everywhere(block, sizes)
    clips = everyone.shape[0]
    audios = everyone[:, :lines].reshape(clips, width)
    texts = everyone[:, lines : 2 * lines].reshape(clips, width)
    flags = everyone[:, 2 * lines, 0]
    picks = everyone[:, 2 * lines, 1 : 2 + negatives.shape[1]].astype(jnp.int32)
    coeff = INV_TEMP / width
    places = jnp.arange(clips, dtype=jnp.int32)
    onehot = (picks[:, :, None] == places[None, None, :]).astype(jnp.float32)
    cross = coeff * jnp.einsum("cd,td->ct", audios, texts, precision=HIGH)
    sims = jnp.sum(onehot * cross[:, None, :], axis=2)
    total = jax.nn.logsumexp(sims, axis=1, keepdims=True)
    weights = CON_WEIGHT * (1.0 - flags)[:, None]
    first_pick = (jnp.arange(sims.shape[1]) == 0).astype(jnp.float32)[None, :]
    d_sims = weights * (jnp.exp(sims - total) - first_pick)
    d_cross = coeff * jnp.sum(onehot * d_sims[:, :, None], axis=1)
    is_me = (places == me).astype(jnp.float32)
    d_audio_vec = jnp.dot(jnp.sum(d_cross * is_me[:, None], axis=0), texts, precision=HIGH)
    d_text_vec = jnp.dot(jnp.sum(d_cross * is_me[None, :], axis=1), audios, precision=HIGH)
    con = jnp.sum((total[:, 0] - sims[:, 0]) * is_me)
    return (d_audio_vec, d_text_vec, con)


def body(
    sizes,
    latent,
    noise,
    text,
    steps,
    empty,
    negatives,
    latent_in,
    time_proj,
    text_proj,
    attn_qkv,
    attn_out,
    glu_in,
    glu_out,
    latent_out,
    norm_gains,
    first_latent_in,
    first_time_proj,
    first_text_proj,
    first_attn_qkv,
    first_attn_out,
    first_glu_in,
    first_glu_out,
    first_latent_out,
    first_norm_gains,
    second_latent_in,
    second_time_proj,
    second_text_proj,
    second_attn_qkv,
    second_attn_out,
    second_glu_in,
    second_glu_out,
    second_latent_out,
    second_norm_gains,
):
    masters = (
        latent_in,
        time_proj,
        text_proj,
        attn_qkv,
        attn_out,
        glu_in,
        glu_out,
        latent_out,
        norm_gains,
    )
    firsts = (
        first_latent_in,
        first_time_proj,
        first_text_proj,
        first_attn_qkv,
        first_attn_out,
        first_glu_in,
        first_glu_out,
        first_latent_out,
        first_norm_gains,
    )
    seconds = (
        second_latent_in,
        second_time_proj,
        second_text_proj,
        second_attn_qkv,
        second_attn_out,
        second_glu_in,
        second_glu_out,
        second_latent_out,
        second_norm_gains,
    )
    weights = gather_weights(masters)
    step_id = steps[0]
    flag = empty[0]
    place = (step_id.astype(jnp.float32) + 0.5) / NB
    alpha = jnp.cos(0.5 * jnp.pi * place)
    sigma = jnp.sin(0.5 * jnp.pi * place)
    clean = latent[0]
    fresh = noise[0]
    noisy = alpha * clean + sigma * fresh
    target = alpha * fresh - sigma * clean
    feats = time_features(step_id)
    words_in = text[0]
    pred, kept, words, audio = layer_forward(weights, noisy, feats, words_in, flag)
    error = pred - target
    frame_n, chans = pred.shape
    mse = jnp.sum(error * error) / (frame_n * chans)
    d_pred = 2.0 * error / (frame_n * chans)
    audio_vec, pull_audio = jax.vjp(unit_scale, jnp.mean(audio, 0))
    text_vec, pull_text = jax.vjp(unit_scale, jnp.mean(words, 0))
    d_audio_vec, d_text_vec, con = contrast(audio_vec, text_vec, empty, negatives, sizes)
    weight = CON_WEIGHT * (1 - flag).astype(jnp.float32)
    d_audio_extra = pull_audio(d_audio_vec)[0][None, :] / frame_n
    d_words_extra = pull_text(d_text_vec)[0][None, :] / words.shape[0]
    pairs, small = layer_backward(weights, kept, words_in, d_pred, d_audio_extra, d_words_extra)
    shares = scatter_grads(pairs, small, masters, sizes)
    squares = jnp.zeros((), jnp.float32)
    for share in shares:
        squares = squares + jnp.sum(share * share)
    loss_local = mse + weight * con
    bucket_local = (jnp.arange(NB, dtype=jnp.int32) == step_id).astype(jnp.float32) * mse
    line = jnp.concatenate([loss_local[None], squares[None], bucket_local])
    line = jnp.pad(line, (0, LANES - line.shape[0]))[None]
    sums = sum_everywhere(jnp.pad(line, ((0, 7), (0, 0))), sizes)[0]
    loss_sum, total_sq, bucket_sums = sums[0], sums[1], sums[2 : 2 + NB]
    grad_norm = jnp.sqrt(total_sq)
    scale = jnp.minimum(1.0, CLIP_NORM / (grad_norm + 1e-06))
    new_weights, new_firsts, new_seconds = ([], [], [])
    for index, (master, first, second, share) in enumerate(zip(masters, firsts, seconds, shares)):
        rate = GAIN_RATE if index == len(masters) - 1 else RATE
        grad = share * scale
        first = BETA_ONE * first + (1.0 - BETA_ONE) * grad
        second = BETA_TWO * second + (1.0 - BETA_TWO) * grad * grad
        fixed_first = first / (1.0 - BETA_ONE**STEP)
        fixed_second = second / (1.0 - BETA_TWO**STEP)
        master = master - rate * (
            fixed_first / (jnp.sqrt(fixed_second) + ADAM_EPS) + DECAY * master
        )
        new_weights.append(master)
        new_firsts.append(first)
        new_seconds.append(second)
    return (
        loss_sum,
        bucket_sums,
        grad_norm,
        new_weights[0],
        new_weights[1],
        new_weights[2],
        new_weights[3],
        new_weights[4],
        new_weights[5],
        new_weights[6],
        new_weights[7],
        new_weights[8],
        new_firsts[0],
        new_firsts[1],
        new_firsts[2],
        new_firsts[3],
        new_firsts[4],
        new_firsts[5],
        new_firsts[6],
        new_firsts[7],
        new_firsts[8],
        new_seconds[0],
        new_seconds[1],
        new_seconds[2],
        new_seconds[3],
        new_seconds[4],
        new_seconds[5],
        new_seconds[6],
        new_seconds[7],
        new_seconds[8],
    )


def solution(mesh):
    sizes = (mesh.shape["dp"], mesh.shape["fsdp"])
    return jax.shard_map(
        functools.partial(body, sizes),
        mesh=mesh,
        in_specs=(
            P(("dp", "fsdp"), None, None),
            P(("dp", "fsdp"), None, None),
            P(("dp", "fsdp"), None, None),
            P(("dp", "fsdp")),
            P(("dp", "fsdp")),
            P(("dp", "fsdp"), None),
            P(None, ("dp", "fsdp")),
            P(("dp", "fsdp"), None),
            P(("dp", "fsdp"), None),
            P(("dp", "fsdp"), None),
            P(("dp", "fsdp"), None),
            P(("dp", "fsdp"), None),
            P(("dp", "fsdp"), None),
            P(("dp", "fsdp"), None),
            P(None, ("dp", "fsdp")),
            P(None, ("dp", "fsdp")),
            P(("dp", "fsdp"), None),
            P(("dp", "fsdp"), None),
            P(("dp", "fsdp"), None),
            P(("dp", "fsdp"), None),
            P(("dp", "fsdp"), None),
            P(("dp", "fsdp"), None),
            P(("dp", "fsdp"), None),
            P(None, ("dp", "fsdp")),
            P(None, ("dp", "fsdp")),
            P(("dp", "fsdp"), None),
            P(("dp", "fsdp"), None),
            P(("dp", "fsdp"), None),
            P(("dp", "fsdp"), None),
            P(("dp", "fsdp"), None),
            P(("dp", "fsdp"), None),
            P(("dp", "fsdp"), None),
            P(None, ("dp", "fsdp")),
        ),
        out_specs=(
            P(),
            P(),
            P(),
            P(None, ("dp", "fsdp")),
            P(("dp", "fsdp"), None),
            P(("dp", "fsdp"), None),
            P(("dp", "fsdp"), None),
            P(("dp", "fsdp"), None),
            P(("dp", "fsdp"), None),
            P(("dp", "fsdp"), None),
            P(("dp", "fsdp"), None),
            P(None, ("dp", "fsdp")),
            P(None, ("dp", "fsdp")),
            P(("dp", "fsdp"), None),
            P(("dp", "fsdp"), None),
            P(("dp", "fsdp"), None),
            P(("dp", "fsdp"), None),
            P(("dp", "fsdp"), None),
            P(("dp", "fsdp"), None),
            P(("dp", "fsdp"), None),
            P(None, ("dp", "fsdp")),
            P(None, ("dp", "fsdp")),
            P(("dp", "fsdp"), None),
            P(("dp", "fsdp"), None),
            P(("dp", "fsdp"), None),
            P(("dp", "fsdp"), None),
            P(("dp", "fsdp"), None),
            P(("dp", "fsdp"), None),
            P(("dp", "fsdp"), None),
            P(None, ("dp", "fsdp")),
        ),
        check_vma=False,
    )
```

```python
import functools
import math

import jax
import jax.numpy as jnp
from jax import lax
from jax.experimental import pallas as pl
from jax.experimental.pallas import tpu as pltpu
from jax.sharding import PartitionSpec as P

AXES = ("dp", "fsdp")
MESH = pl.DeviceIdType.MESH
LANES = 128
COLS = 256
LAGS = (2, 2, 2, 2, 2)
SLOTS = 6
KEPT = 2
PLACES = (("x", "dp", 2), ("core", "dp", 1), ("z1", "fsdp", 4), ("z0", "fsdp", 2), ("y", "fsdp", 1))
ORDERS = (
    ("z1", "z0", "y", "x", "core"),
    ("z1", "z0", "x", "y", "core"),
    ("z1", "z0", "y", "x", "core"),
    ("z1", "z0", "x", "y", "core"),
    ("x", "y", "z1", "z0", "core"),
)
HELD = 20
SPREAD_LAGS = (2, 2, 3, 3, 2)

HD = 64
TF = 256
NB = 8
STEP = 10


EPS_NORM = 1e-05
BETA_ONE = 0.9
BETA_TWO = 0.95
ADAM_EPS = 1e-08
RATE = 0.02
GAIN_RATE = 0.3
DECAY = 0.01
CLIP_NORM = 0.05
CON_WEIGHT = 0.5
INV_TEMP = 50.0
HIGH = lax.Precision.HIGHEST


def matmul(left, right):
    return jnp.dot(left, right, preferred_element_type=jnp.float32)


def matmul_tn(left, right):
    return lax.dot_general(
        left, right, (((0,), (0,)), ((), ())), preferred_element_type=jnp.float32
    )


def matmul_nt(left, right):
    return lax.dot_general(
        left, right, (((1,), (1,)), ((), ())), preferred_element_type=jnp.float32
    )


def layer_norm(x, gain):
    cent = x - jnp.mean(x, axis=-1, keepdims=True)
    var = jnp.mean(cent * cent, axis=-1, keepdims=True)
    return cent * lax.rsqrt(var + EPS_NORM) * gain


def norm_back(x, gain, grad):
    _, pull = jax.vjp(layer_norm, x, gain)
    return pull(grad)


def unit_scale(x):
    return x * lax.rsqrt(jnp.mean(x * x) + EPS_NORM)


def time_features(step_id):
    place = (step_id.astype(jnp.float32) + 0.5) / NB
    half = TF // 2
    freqs = jnp.exp(jnp.arange(half, dtype=jnp.float32) * (math.log(100.0) / half))
    angle = place * freqs
    return jnp.concatenate([jnp.cos(angle), jnp.sin(angle)])


def attention_probs(query, keys, keep, lse_rows):
    scores = jnp.einsum("qhd,khd->hqk", query, keys, preferred_element_type=jnp.float32) * HD ** (
        -0.5
    )
    scores = jnp.where(keep[None, None, :], scores, -1e30)
    if lse_rows is None:
        top = jnp.max(scores, axis=-1, keepdims=True)
        lse_rows = top + jnp.log(jnp.sum(jnp.exp(scores - top), axis=-1, keepdims=True))
    return (jnp.exp(scores - lse_rows), lse_rows)


def layer_forward(weights, gu_share, sizes, noisy, feats, words_in, flag):
    lat_w, time_w, text_w, qkv_w, out_w, down_w, lout_w, gains = weights
    gains = gains.astype(jnp.float32)
    frame_n = noisy.shape[0]
    noisy_b = noisy.astype(jnp.bfloat16)
    feats_b = feats.astype(jnp.bfloat16)[None]
    frames = matmul(noisy_b, lat_w) + matmul(feats_b, time_w)
    words = matmul(words_in, text_w)
    hidden = jnp.concatenate([frames, words], 0)
    seq, width = hidden.shape
    heads = width // HD
    normed_b = layer_norm(hidden, gains[0]).astype(jnp.bfloat16)
    qkv = matmul(normed_b, qkv_w).astype(jnp.bfloat16)
    query = qkv[:frame_n, :width].reshape(frame_n, heads, HD)
    keys = qkv[:, width : 2 * width].reshape(seq, heads, HD)
    values = qkv[:, 2 * width :].reshape(seq, heads, HD)
    keep = (jnp.arange(seq) < frame_n) | (flag == 0)
    probs, lse_rows = attention_probs(query, keys, keep, None)
    mixed_b = (
        jnp.einsum(
            "hqk,khd->qhd", probs.astype(jnp.bfloat16), values, preferred_element_type=jnp.float32
        )
        .reshape(frame_n, width)
        .astype(jnp.bfloat16)
    )
    after = frames + matmul(mixed_b, out_w)
    normed2_b = layer_norm(after, gains[1]).astype(jnp.bfloat16)
    gu_w, gate_up = up_project(normed2_b, gu_share, sizes)
    ffw = gate_up.shape[1] // 2
    gate = gate_up[:, :ffw].astype(jnp.float32)
    up = gate_up[:, ffw:].astype(jnp.float32)
    inner_b = (jax.nn.silu(gate) * up).astype(jnp.bfloat16)
    final = after + matmul(inner_b, down_w)
    audio = final
    out_b = layer_norm(audio, gains[2]).astype(jnp.bfloat16)
    pred = matmul(out_b, lout_w)
    kept = (
        noisy_b,
        feats,
        hidden,
        normed_b,
        qkv,
        keep,
        lse_rows,
        mixed_b,
        after,
        normed2_b,
        gate_up,
        inner_b,
        audio,
        out_b,
    )
    return (pred, kept, words, audio, gu_w)


def layer_backward(weights, gu_w, kept, words_in, d_pred, d_audio_extra, d_words_extra):
    lat_w, time_w, text_w, qkv_w, out_w, down_w, lout_w, gains = weights
    gains = gains.astype(jnp.float32)
    (
        noisy_b,
        feats,
        hidden,
        normed_b,
        qkv,
        keep,
        lse_rows,
        mixed_b,
        after,
        normed2_b,
        gate_up,
        inner_b,
        audio,
        out_b,
    ) = kept
    frame_n = audio.shape[0]
    seq, width = hidden.shape
    heads = width // HD
    d_pred_b = d_pred.astype(jnp.bfloat16)
    g_lout = matmul_tn(out_b, d_pred_b)
    d_audio, g_gain2 = norm_back(audio, gains[2], matmul_nt(d_pred_b, lout_w))
    d_final = d_audio + d_audio_extra
    d_final_b = d_final.astype(jnp.bfloat16)
    d_inner = matmul_nt(d_final_b, down_w)
    ffw = gate_up.shape[1] // 2
    gate = gate_up[:, :ffw].astype(jnp.float32)
    up = gate_up[:, ffw:].astype(jnp.float32)
    sig = jax.nn.sigmoid(gate)
    d_gate = d_inner * up * (sig * (1.0 + gate * (1.0 - sig)))
    d_up = d_inner * (gate * sig)
    d_gate_b, d_up_b = lax.optimization_barrier(
        (d_gate.astype(jnp.bfloat16), d_up.astype(jnp.bfloat16))
    )
    d_gu_b = jnp.concatenate([d_gate_b, d_up_b], 1)
    d_after_n, g_gain1 = norm_back(after, gains[1], matmul_nt(d_gu_b, gu_w))
    d_after = d_final + d_after_n
    d_after_b = d_after.astype(jnp.bfloat16)
    d_mixed_b = matmul_nt(d_after_b, out_w).astype(jnp.bfloat16)
    d_mixed_b = d_mixed_b.reshape(frame_n, heads, HD)
    query = qkv[:frame_n, :width].reshape(frame_n, heads, HD)
    keys = qkv[:, width : 2 * width].reshape(seq, heads, HD)
    values = qkv[:, 2 * width :].reshape(seq, heads, HD)
    probs, _ = attention_probs(query, keys, keep, lse_rows)
    d_probs = jnp.einsum("qhd,khd->hqk", d_mixed_b, values, preferred_element_type=jnp.float32)
    d_values = jnp.einsum(
        "hqk,qhd->khd", probs.astype(jnp.bfloat16), d_mixed_b, preferred_element_type=jnp.float32
    )
    d_scores_b = (probs * (d_probs - jnp.sum(probs * d_probs, axis=-1, keepdims=True))).astype(
        jnp.bfloat16
    )
    d_query = jnp.einsum(
        "hqk,khd->qhd", d_scores_b, keys, preferred_element_type=jnp.float32
    ) * HD ** (-0.5)
    d_keys = jnp.einsum(
        "hqk,qhd->khd", d_scores_b, query, preferred_element_type=jnp.float32
    ) * HD ** (-0.5)
    d_qkv_b = jnp.concatenate(
        [
            jnp.pad(d_query.reshape(frame_n, width), ((0, seq - frame_n), (0, 0))),
            d_keys.reshape(seq, width),
            d_values.reshape(seq, width),
        ],
        1,
    ).astype(jnp.bfloat16)
    d_hidden_n, g_gain0 = norm_back(hidden, gains[0], matmul_nt(d_qkv_b, qkv_w))
    d_frames_b = (d_after + d_hidden_n[:frame_n]).astype(jnp.bfloat16)
    d_words_b = (d_hidden_n[frame_n:] + d_words_extra).astype(jnp.bfloat16)
    g_lat = matmul_tn(d_frames_b, noisy_b)
    column = jnp.sum(d_frames_b.astype(jnp.float32), 0)
    feats_low = lax.reduce_precision(feats, 8, 7)
    g_text = matmul_tn(words_in, d_words_b)
    g_gains = jnp.stack([g_gain0, g_gain1, g_gain2])
    lefts = (normed2_b, inner_b, mixed_b, normed_b)
    rights = (d_gate_b, d_up_b, d_final_b, d_after_b, d_qkv_b)
    return (lefts, rights, (g_lat, column, feats_low, g_text, g_lout, g_gains))


def mine(axis, bit):
    return lax.rem(lax.axis_index(axis) // bit, 2)


def partner(axis, bit):
    return {axis: lax.axis_index(axis) + bit * (1 - 2 * mine(axis, bit))}


def greet(steps):
    barrier = pltpu.get_barrier_semaphore()
    for axis, bit in steps:
        pl.semaphore_signal(barrier, inc=1, device_id=partner(axis, bit), device_id_type=MESH)
    pl.semaphore_wait(barrier, len(steps))


def gather_kernel(sizes, block_ref, all_ref, send_sem, recv_sem):
    dp_size, fsdp_size = sizes
    dp, fsdp = lax.axis_index("dp"), lax.axis_index("fsdp")
    rounds = (("fsdp", fsdp, fsdp_size, 1), ("dp", dp, dp_size, fsdp_size))
    barrier = pltpu.get_barrier_semaphore()
    for axis, place, size, _ in rounds:
        for hop in range(1, size):
            peer = {axis: lax.rem(place + hop, size)}
            pl.semaphore_signal(barrier, inc=1, device_id=peer, device_id_type=MESH)
    pl.semaphore_wait(barrier, dp_size + fsdp_size - 2)
    all_ref[pl.ds(dp * fsdp_size + fsdp, 1)] = block_ref[...][None]
    first = 0
    for axis, place, size, span in rounds:

        def copy(hop, owner):
            start = dp * fsdp_size + owner if axis == "fsdp" else owner * fsdp_size
            held = all_ref.at[pl.ds(start, span)]
            return pltpu.make_async_remote_copy(
                src_ref=held,
                dst_ref=held,
                send_sem=send_sem.at[first + hop - 1],
                recv_sem=recv_sem.at[first + hop - 1],
                device_id={axis: lax.rem(place + hop, size)},
                device_id_type=MESH,
            )

        for hop in range(1, size):
            copy(hop, place).start()
        for hop in range(1, size):
            copy(hop, lax.rem(place + size - hop, size)).wait_recv()
            copy(hop, place).wait_send()
        first += size - 1


def gather_everywhere(block, sizes):
    count = sizes[0] + sizes[1] - 2
    return pl.pallas_call(
        functools.partial(gather_kernel, sizes),
        out_shape=jax.ShapeDtypeStruct((sizes[0] * sizes[1],) + block.shape, block.dtype),
        in_specs=[pl.BlockSpec(memory_space=pltpu.VMEM)],
        out_specs=pl.BlockSpec(memory_space=pltpu.VMEM),
        scratch_shapes=[pltpu.SemaphoreType.DMA((count,)), pltpu.SemaphoreType.DMA((count,))],
        compiler_params=pltpu.CompilerParams(collective_id=0, has_side_effects=True),
    )(block)


def scatter_kernel(plan, *refs):
    rows, folds = plan["rows"], plan["folds"]
    (xt_gu, xt_down, xt_out, xt_qkv, *rest) = refs
    (dy_gate, dy_up, dy_down, dy_out, dy_qkv, text, time, small, line, *rest) = rest
    (o_gu, o_down, o_out, o_qkv, o_text, o_time, o_small, o_line, *rest) = rest
    (xs, xq, dya, dyq, ss, rr, kk, final, squares, part, came, *rest) = rest
    (load_sem, dy_sem, misc_sem, send_sem, recv_sem, out_sem, line_sem) = rest
    wide = [d.shape[1] // COLS for d in (dy_gate, dy_up, dy_down, dy_out, dy_qkv)]
    wide[2] *= folds
    wide += [text.shape[1] // (2 * COLS), time.shape[1] // COLS, small.shape[1] // COLS]
    ends = [sum(wide[: i + 1]) for i in range(len(wide))]
    starts = [0] + ends[:-1]
    total = ends[-1]
    first_q, first_misc = starts[4], starts[5]
    per_fold = wide[2] // folds
    stages = (("dp", 1), ("dp", 2), ("fsdp", 1), ("fsdp", 2), ("fsdp", 4))
    after = [sum(LAGS[:k]) for k in range(6)]
    greet(stages)

    dp, fsdp = lax.axis_index("dp"), lax.axis_index("fsdp")
    core, x = lax.rem(dp, 2), dp // 2
    y, z0, z1 = lax.rem(fsdp, 2), lax.rem(fsdp // 2, 2), fsdp // 4

    def owner(block):
        def bit(own, weight):
            same = lax.rem(block // weight, 2)
            return own + (1 - same) * (1 - 2 * own)

        where = bit(x, 8) * 2 + bit(core, 16)
        return where * 8 + bit(z1, 1) * 4 + bit(z0, 2) * 2 + bit(y, 4)

    def load(source, fold, dest, index, reach):
        def one(block, carry):
            first = pl.multiple_of(owner(block) * (reach * rows) + fold * rows, 16)
            pltpu.make_async_copy(
                source.at[pl.ds(first, rows)], dest.at[block], load_sem.at[index]
            ).start()
            return carry

        lax.fori_loop(0, 32, one, 0)

    load(xt_gu, 0, xs.at[0], 0, 1)
    for fold in range(folds):
        load(xt_down, fold, xs.at[1 + fold], 1 + fold, folds)
    load(xt_out, 0, xs.at[1 + folds], 1 + folds, 1)
    load(xt_qkv, 0, xq, 2 + folds, 1)

    def columns(tile):
        return pl.ds(pl.multiple_of(tile * COLS, COLS), COLS)

    def within(tile, low, high):
        return (tile >= low) & (tile < high)

    def fetch(tile):
        slot = lax.rem(tile, 2)
        for index, source in enumerate((dy_gate, dy_up, dy_down, dy_out, dy_qkv)):
            dest = dya if index < 4 else dyq

            @pl.when(within(tile, starts[index], ends[index]))
            def _(index=index, source=source, dest=dest):
                place = lax.rem(tile - starts[index], source.shape[1] // COLS)
                pltpu.make_async_copy(
                    source.at[:, columns(place)], dest.at[slot], dy_sem.at[slot]
                ).start()

    def product(left, right, half, keep):
        def some(step, carry):
            lhs = left[pl.ds(half * 16 + step * 4, 4)]
            out = jnp.dot(
                lhs.reshape(4 * rows, lhs.shape[-1]), right[...], preferred_element_type=jnp.float32
            )
            keep[pl.ds(pl.multiple_of(step * 4, 4), 4)] = out.reshape(4, rows, COLS)
            return carry

        lax.fori_loop(0, 4, some, 0)

    def copy(stage, parity, tile):
        axis, bit = stages[stage]
        if parity and stage in (1, 2):
            axis, bit = stages[3 - stage]
        slot = lax.rem(tile, SLOTS)
        return pltpu.make_async_remote_copy(
            src_ref=ss[stage].at[slot],
            dst_ref=rr[stage].at[slot],
            send_sem=send_sem.at[stage, slot],
            recv_sem=recv_sem.at[stage, slot],
            device_id=partner(axis, bit),
            device_id_type=MESH,
        )

    def out_copies(tile):
        slot = lax.rem(tile, 2)
        half = rows // 2
        for index, dest in enumerate(
            (o_gu, o_gu, o_down, o_out, o_qkv, o_text, o_time, o_small)
        ):

            @pl.when(within(tile, starts[index], ends[index]))
            def _(index=index, dest=dest):
                place, row = tile - starts[index], 0
                if index == 1:
                    place = place + wide[0]
                if index == 2:
                    row = pl.multiple_of((place // per_fold) * rows, 8)
                    place = lax.rem(place, per_fold)
                if index == 5:
                    for side in range(2):
                        pltpu.make_async_copy(
                            final.at[slot, pl.ds(side * half, half)],
                            dest.at[:, columns(side * wide[5] + place)],
                            out_sem.at[slot],
                        ).start()
                else:
                    pltpu.make_async_copy(
                        final.at[slot], dest.at[pl.ds(row, rows), columns(place)], out_sem.at[slot]
                    ).start()

    def wait_out(tile):
        slot = lax.rem(tile, 2)
        pltpu.make_async_copy(final.at[slot], o_gu.at[:, columns(0)], out_sem.at[slot]).wait()

    def freed(stage, parity, tile):
        @pl.when((tile >= SLOTS) & (tile < total + SLOTS) & (lax.rem(tile, 2) == parity))
        def _():
            copy(stage, parity, tile - SLOTS).wait_send()

    def make(tile):
        freed(0, 0, tile)
        freed(0, 1, tile)

        @pl.when(tile < total)
        def _():
            side = lax.rem(tile, 2)
            send, keep = ss[0].at[lax.rem(tile, SLOTS)], kk[0].at[lax.rem(tile, KEPT)]

            @pl.when(tile + 1 < first_misc)
            def _():
                fetch(tile + 1)

            @pl.when(tile < first_q)
            def _():
                pltpu.make_async_copy(dy_gate.at[:, columns(0)], dya.at[side], dy_sem.at[side]).wait()
                fold = (tile - starts[2]) // per_fold
                which = jnp.where(tile >= ends[2], 1 + folds, 1 + fold)
                left = xs.at[jnp.where(tile < starts[2], 0, which)]
                product(left, dya.at[side], 0, send)
                copy(0, 0, tile).start()
                product(left, dya.at[side], 1, keep)

            @pl.when(within(tile, first_q, first_misc))
            def _():
                pltpu.make_async_copy(dy_qkv.at[:, columns(0)], dyq.at[side], dy_sem.at[side]).wait()
                product(xq, dyq.at[side], 0, send)
                copy(0, 0, tile).start()
                product(xq, dyq.at[side], 1, keep)

            @pl.when(tile >= first_misc)
            def _():
                def one(block, carry):
                    for index, dest in enumerate((send, keep)):
                        who = owner(block + 16 * index)

                        def bring(source, row, place, low, count, dest=dest, index=index):
                            pltpu.make_async_copy(
                                source.at[pl.ds(pl.multiple_of(row, 8), count), columns(place)],
                                dest.at[block, pl.ds(low, count)],
                                misc_sem.at[index],
                            ).start()

                        @pl.when(tile < ends[5])
                        def _():
                            half = rows // 2
                            for part_of in range(2):
                                place = part_of * wide[5] + tile - starts[5]
                                bring(text, who * half, place, part_of * half, half)

                        @pl.when(within(tile, starts[6], ends[6]))
                        def _():
                            bring(time, who * rows, tile - starts[6], 0, rows)

                        @pl.when(tile >= starts[7])
                        def _():
                            bring(small, who * rows, tile - starts[7], 0, rows)

                    return carry

                lax.fori_loop(0, 16, one, 0)
                pltpu.make_async_copy(send, send, misc_sem.at[0]).wait()
                copy(0, 0, tile).start()
                pltpu.make_async_copy(keep, keep, misc_sem.at[1]).wait()

    def pass_on(stage, parity, tile):
        freed(stage, parity, tile)

        @pl.when(within(tile, 0, total) & (lax.rem(tile, 2) == parity))
        def _():
            slot = lax.rem(tile, SLOTS)
            copy(stage - 1, parity, tile).wait_recv()
            came_in, held = rr[stage - 1].at[slot], kk[stage - 1].at[lax.rem(tile, KEPT)]
            send, keep = ss[stage].at[slot], kk[stage].at[lax.rem(tile, KEPT)]
            half = 32 >> (stage + 1)
            group = half // 2 if (stage == 1 and parity) else half

            def first(block, carry):
                low = block + (block // group) * group
                send[block] = (held[low] + came_in[low].astype(jnp.float32)).astype(send.dtype)
                return carry

            def second(block, carry):
                high = block + (block // group) * group + group
                keep[block] = held[high] + came_in[high].astype(jnp.float32)
                return carry

            lax.fori_loop(0, half, first, 0)
            copy(stage, parity, tile).start()
            lax.fori_loop(0, half, second, 0)

    def finish(tile):
        @pl.when(within(tile, 2, total + 2))
        def _():
            wait_out(tile)

        @pl.when(within(tile, 0, total))
        def _():
            copy(4, 0, tile).wait_recv()
            held, came_in = kk[4].at[lax.rem(tile, KEPT)], rr[4].at[lax.rem(tile, SLOTS)]
            sums = held[0] + came_in[0].astype(jnp.float32)
            final[lax.rem(tile, 2)] = sums
            squares[...] += sums * sums
            out_copies(tile)

    squares[...] = jnp.zeros_like(squares)
    fetch(0)
    for index in range(3 + folds):
        dest = xq if index == 2 + folds else xs.at[index]
        pltpu.make_async_copy(dest, dest, load_sem.at[index]).wait()

    def step(now, carry):
        finish(now - after[5])
        for stage in (4, 3, 2, 1):
            pass_on(stage, 0, now - after[stage])
            pass_on(stage, 1, now - after[stage])
        make(now)
        return carry

    lax.fori_loop(0, total + max(after[5] + 2, after[4] + SLOTS), step, 0)

    row = lax.broadcasted_iota(jnp.int32, line.shape, 0)
    lane = lax.broadcasted_iota(jnp.int32, line.shape, 1)
    part[0] = line[...] + jnp.where((row == 0) & (lane == 1), jnp.sum(squares[...]), 0.0)
    for index, (axis, bit) in enumerate(stages):
        swap = pltpu.make_async_remote_copy(
            src_ref=part.at[index],
            dst_ref=came.at[index],
            send_sem=line_sem.at[0, index],
            recv_sem=line_sem.at[1, index],
            device_id=partner(axis, bit),
            device_id_type=MESH,
        )
        swap.start()
        swap.wait()
        part[index + 1] = part[index] + came[index]
    o_line[...] = part[len(stages)]


def scatter_sums(xts, dys, misc, line):
    xt_gu, xt_down, xt_out, xt_qkv = xts
    dy_gate, dy_up, dy_down, dy_out, dy_qkv = dys
    text, time, small = misc
    rows = xt_gu.shape[0] // 32
    folds = xt_down.shape[0] // xt_gu.shape[0]
    plan = {"rows": rows, "folds": folds}
    sizes = [16 >> stage for stage in range(5)]
    f32, bf16 = jnp.float32, jnp.bfloat16
    link_types = (f32, bf16, bf16, f32, f32)
    scratch = [
        pltpu.VMEM((2 + folds, 32, rows, xt_gu.shape[1]), bf16),
        pltpu.VMEM((32, rows, xt_qkv.shape[1]), bf16),
        pltpu.VMEM((2, xt_gu.shape[1], COLS), bf16),
        pltpu.VMEM((2, xt_qkv.shape[1], COLS), bf16),
        [pltpu.VMEM((SLOTS, n, rows, COLS), t) for n, t in zip(sizes, link_types)],
        [pltpu.VMEM((SLOTS, n, rows, COLS), t) for n, t in zip(sizes, link_types)],
        [pltpu.VMEM((KEPT, n, rows, COLS), f32) for n in sizes],
        pltpu.VMEM((2, rows, COLS), f32),
        pltpu.VMEM((rows, COLS), f32),
        pltpu.VMEM((6,) + line.shape, f32),
        pltpu.VMEM((5,) + line.shape, f32),
        pltpu.SemaphoreType.DMA((3 + folds,)),
        pltpu.SemaphoreType.DMA((2,)),
        pltpu.SemaphoreType.DMA((2,)),
        pltpu.SemaphoreType.DMA((5, SLOTS)),
        pltpu.SemaphoreType.DMA((5, SLOTS)),
        pltpu.SemaphoreType.DMA((2,)),
        pltpu.SemaphoreType.DMA((2, 5)),
    ]

    def out(height, width):
        return jax.ShapeDtypeStruct((height, width), f32)

    width = dy_down.shape[1]
    outs = [
        out(rows, dy_gate.shape[1] + dy_up.shape[1]),
        out(rows * folds, width),
        out(rows, width),
        out(rows, dy_qkv.shape[1]),
        out(rows // 2, text.shape[1]),
        out(rows, time.shape[1]),
        out(rows, small.shape[1]),
        jax.ShapeDtypeStruct(line.shape, f32),
    ]
    in_hbm = pl.BlockSpec(memory_space=pl.ANY)
    in_vmem = pl.BlockSpec(memory_space=pltpu.VMEM)
    return pl.pallas_call(
        functools.partial(scatter_kernel, plan),
        out_shape=outs,
        in_specs=[in_hbm] * 12 + [in_vmem],
        out_specs=[in_hbm] * 7 + [in_vmem],
        scratch_shapes=scratch,
        compiler_params=pltpu.CompilerParams(
            collective_id=2, has_side_effects=True, vmem_limit_bytes=56 * 1024 * 1024
        ),
    )(*xts, *dys, *misc, line)


def spread_kernel(total, multiply, *refs):
    if multiply:
        (share, left, full, product, whole, result, send_sem, recv_sem, full_sem, out_sem) = refs
    else:
        (share, early, full, late, whole, send_sem, recv_sem, full_sem, late_sem) = refs
        hand_on = pltpu.make_async_copy(early, late, late_sem)
        hand_on.start()
    greet([(axis, bit) for _, axis, bit in PLACES])
    after = [sum(SPREAD_LAGS[:k]) for k in range(6)]
    mine_at = {name: mine(axis, bit) for name, axis, bit in PLACES}
    links_of = {name: (axis, bit) for name, axis, bit in PLACES}

    def columns(tile):
        return pl.ds(pl.multiple_of(tile * COLS, COLS), COLS)

    def held(order, stage, slot):
        done = order[:stage]
        where = tuple(slice(None) if n in done else mine_at[n] for n, _, _ in PLACES)
        return whole.at[(slot,) + where]

    def copy(order, stage, tile):
        slot = lax.rem(tile, HELD)
        group = held(order, stage, slot)
        return pltpu.make_async_remote_copy(
            src_ref=group,
            dst_ref=group,
            send_sem=send_sem.at[stage, slot],
            recv_sem=recv_sem.at[stage, slot],
            device_id=partner(*links_of[order[stage]]),
            device_id_type=MESH,
        )

    def each_order(tile, act):
        for kind, order in enumerate(ORDERS):

            @pl.when((tile >= 0) & (tile < total) & (lax.rem(tile, len(ORDERS)) == kind))
            def _(order=order):
                act(order)

    def write(tile):
        slot = lax.rem(tile, HELD)
        return pltpu.make_async_copy(
            whole.at[slot], full.at[:, :, :, :, :, :, columns(tile)], full_sem.at[lax.rem(tile, 2)]
        )

    def give(tile):
        slot = lax.rem(tile, 2)
        return pltpu.make_async_copy(
            result.at[slot], product.at[:, columns(tile)], out_sem.at[slot]
        )

    def step(now, carry):
        last = now - after[5]

        @pl.when((last >= 1) & (last <= total))
        def _():
            write(last - 1).wait()

        def end(order):
            for stage in range(5):
                copy(order, stage, last).wait_send()
            copy(order, 4, last).wait_recv()

        each_order(last, end)

        @pl.when((last >= 0) & (last < total))
        def _():
            write(last).start()
            if multiply:

                @pl.when(last >= 2)
                def _():
                    give(last - 2).wait()

                tile = whole[lax.rem(last, HELD)]
                result[lax.rem(last, 2)] = jnp.dot(
                    left[...],
                    tile.reshape(left.shape[1], COLS),
                    preferred_element_type=jnp.float32,
                ).astype(result.dtype)
                give(last).start()

        for stage in (4, 3, 2, 1):
            tile = now - after[stage]

            def onward(order, stage=stage, tile=tile):
                copy(order, stage - 1, tile).wait_recv()
                copy(order, stage, tile).start()

            each_order(tile, onward)

        @pl.when(now < total)
        def _():
            place = tuple(mine_at[n] for n, _, _ in PLACES)
            whole[(lax.rem(now, HELD),) + place] = share[:, columns(now)].astype(whole.dtype)

        each_order(now, lambda order: copy(order, 0, now).start())
        return carry

    lax.fori_loop(0, total + after[5] + 1, step, 0)
    if multiply:
        for tile in range(max(total - 2, 0), total):
            give(tile).wait()
    else:
        hand_on.wait()


def spread(share, left, early, identity):
    rows, width = share.shape
    total = width // COLS
    bf16 = jnp.bfloat16
    places = (2,) * 5
    out_shape = [jax.ShapeDtypeStruct(places + (rows, width), bf16)]
    scratch = [pltpu.VMEM((HELD,) + places + (rows, COLS), bf16)]
    sems = [pltpu.SemaphoreType.DMA((5, HELD))] * 2 + [pltpu.SemaphoreType.DMA((2,))]
    in_hbm = pl.BlockSpec(memory_space=pl.ANY)
    in_specs = [pl.BlockSpec(memory_space=pltpu.VMEM)] * 2
    if left is None:
        args = [share, early]
        in_specs[1] = in_hbm
        out_shape.append(jax.ShapeDtypeStruct(early.shape, early.dtype))
        sems.append(pltpu.SemaphoreType.DMA)
    else:
        args = [share, left]
        out_shape.append(jax.ShapeDtypeStruct((left.shape[0], width), bf16))
        scratch.append(pltpu.VMEM((2, left.shape[0], COLS), bf16))
        sems.append(pltpu.SemaphoreType.DMA((2,)))
    results = pl.pallas_call(
        functools.partial(spread_kernel, total, left is not None),
        out_shape=out_shape,
        in_specs=in_specs,
        out_specs=[in_hbm] * 2,
        scratch_shapes=scratch + sems,
        compiler_params=pltpu.CompilerParams(
            collective_id=identity, has_side_effects=True, vmem_limit_bytes=40 * 1024 * 1024
        ),
    )(*args)
    return [results[0].reshape(32 * rows, width)] + list(results[1:])


def fold(share, rows):
    return share.reshape(rows, share.size // rows)


def unstack(stacked, few):
    pieces = stacked.shape[0] // few
    return stacked.reshape(pieces, few, -1).swapaxes(0, 1).reshape(few, -1)


def by_tiles(sizes, rows):
    return sizes == (4, 8) and rows % 16 == 0


def whole_rows(share):
    return lax.all_gather(share.astype(jnp.bfloat16), AXES, axis=0, tiled=True)


def gather_weights(masters, sizes):
    lat, time, text, qkv, out, _, down, lout, gains = masters
    rows, width = out.shape
    gains_t = jnp.pad(gains.T, ((0, 0), (0, LANES - gains.shape[0])))
    pieces = [qkv, out, fold(text, rows), fold(time, rows), lat.T, lout, gains_t]
    packed = jnp.concatenate(pieces, 1).astype(jnp.bfloat16)
    low_down = down.astype(jnp.bfloat16)
    if by_tiles(sizes, rows):
        gathered, low_down = spread(packed, None, low_down, 3)
    else:
        gathered = whole_rows(packed)
    full, start = [], 0
    for piece in pieces:
        full.append(gathered[:, start : start + piece.shape[1]])
        start += piece.shape[1]
    return (
        full[4].T,
        full[3].reshape(-1, width),
        full[2].reshape(-1, width),
        full[0],
        full[1],
        whole_rows(low_down),
        full[5],
        full[6][:, : gains.shape[0]].T,
    )


def up_project(normed, share, sizes):
    if by_tiles(sizes, share.shape[0]):
        return spread(share, normed, None, 4)
    weight = whole_rows(share)
    return (weight, matmul(normed, weight).astype(jnp.bfloat16))


def scatter_grads(lefts, rights, small, masters, line, sizes):
    lat, column, feats, text, lout, gains = small
    rows = masters[3].shape[0]
    few = masters[1].shape[0]
    pieces = rows // few
    time = (
        feats.reshape(-1, 1, few, 1) * column.reshape(1, pieces, 1, column.shape[0] // pieces)
    ).reshape(-1, column.shape[0] // pieces)
    gains_t = jnp.pad(gains.T, ((0, 0), (0, LANES - gains.shape[0])))
    packed = jnp.concatenate([lat, lout, gains_t], 1)
    chans = lat.shape[1]
    if by_tiles(sizes, rows):
        gu, down, out, qkv, g_text, g_time, g_small, line = scatter_sums(
            [x.T for x in lefts], rights, [text, time, packed], line
        )
    else:
        d_gate, d_up, d_final, d_after, d_qkv = rights
        d_gu = jnp.concatenate([d_gate, d_up], 1)
        grads = [matmul_tn(x, d) for x, d in zip(lefts, (d_gu, d_final, d_after, d_qkv))]
        gu, down, out, qkv, g_text, g_time, g_small = sums = [
            lax.psum_scatter(g, AXES, scatter_dimension=0, tiled=True)
            for g in grads + [text, time, packed]
        ]
        squares = sum(jnp.sum(g * g) for g in sums)
        line = lax.psum(line.at[0, 1].set(squares), AXES)
    shares = (
        g_small[:, :chans].T,
        unstack(g_time, few),
        g_text,
        qkv,
        out,
        gu,
        down,
        g_small[:, chans : 2 * chans],
        g_small[:, 2 * chans : 2 * chans + gains.shape[0]].T,
    )
    return (shares, line[0])


def contrast(audio_vec, text_vec, empty, negatives, sizes):
    width = audio_vec.shape[0]
    lines = width // LANES
    me = lax.axis_index(AXES)
    facts = jnp.concatenate([empty, me[None], negatives[0]]).astype(jnp.float32)
    block = jnp.concatenate(
        [
            audio_vec.reshape(lines, LANES),
            lax.reduce_precision(text_vec, 8, 7).reshape(lines, LANES),
            jnp.pad(facts, (0, LANES - facts.shape[0]))[None],
        ]
    )
    block = jnp.pad(block, ((0, -block.shape[0] % 8), (0, 0)))
    everyone = gather_everywhere(block, sizes)
    clips = everyone.shape[0]
    audios = everyone[:, :lines].reshape(clips, width)
    texts = everyone[:, lines : 2 * lines].reshape(clips, width)
    flags = everyone[:, 2 * lines, 0]
    picks = everyone[:, 2 * lines, 1 : 2 + negatives.shape[1]].astype(jnp.int32)
    coeff = INV_TEMP / width
    places = jnp.arange(clips, dtype=jnp.int32)
    onehot = (picks[:, :, None] == places[None, None, :]).astype(jnp.float32)
    cross = coeff * jnp.einsum("cd,td->ct", audios, texts, precision=HIGH)
    sims = jnp.sum(onehot * cross[:, None, :], axis=2)
    total = jax.nn.logsumexp(sims, axis=1, keepdims=True)
    weights = CON_WEIGHT * (1.0 - flags)[:, None]
    first_pick = (jnp.arange(sims.shape[1]) == 0).astype(jnp.float32)[None, :]
    d_sims = weights * (jnp.exp(sims - total) - first_pick)
    d_cross = coeff * jnp.sum(onehot * d_sims[:, :, None], axis=1)
    is_me = (places == me).astype(jnp.float32)
    d_audio_vec = jnp.dot(jnp.sum(d_cross * is_me[:, None], axis=0), texts, precision=HIGH)
    d_text_vec = jnp.dot(jnp.sum(d_cross * is_me[None, :], axis=1), audios, precision=HIGH)
    con = jnp.sum((total[:, 0] - sims[:, 0]) * is_me)
    return (d_audio_vec, d_text_vec, con)


def body(
    sizes,
    latent,
    noise,
    text,
    steps,
    empty,
    negatives,
    latent_in,
    time_proj,
    text_proj,
    attn_qkv,
    attn_out,
    glu_in,
    glu_out,
    latent_out,
    norm_gains,
    first_latent_in,
    first_time_proj,
    first_text_proj,
    first_attn_qkv,
    first_attn_out,
    first_glu_in,
    first_glu_out,
    first_latent_out,
    first_norm_gains,
    second_latent_in,
    second_time_proj,
    second_text_proj,
    second_attn_qkv,
    second_attn_out,
    second_glu_in,
    second_glu_out,
    second_latent_out,
    second_norm_gains,
):
    masters = (
        latent_in,
        time_proj,
        text_proj,
        attn_qkv,
        attn_out,
        glu_in,
        glu_out,
        latent_out,
        norm_gains,
    )
    firsts = (
        first_latent_in,
        first_time_proj,
        first_text_proj,
        first_attn_qkv,
        first_attn_out,
        first_glu_in,
        first_glu_out,
        first_latent_out,
        first_norm_gains,
    )
    seconds = (
        second_latent_in,
        second_time_proj,
        second_text_proj,
        second_attn_qkv,
        second_attn_out,
        second_glu_in,
        second_glu_out,
        second_latent_out,
        second_norm_gains,
    )
    weights = gather_weights(masters, sizes)
    step_id = steps[0]
    flag = empty[0]
    place = (step_id.astype(jnp.float32) + 0.5) / NB
    alpha = jnp.cos(0.5 * jnp.pi * place)
    sigma = jnp.sin(0.5 * jnp.pi * place)
    clean = latent[0]
    fresh = noise[0]
    noisy = alpha * clean + sigma * fresh
    target = alpha * fresh - sigma * clean
    feats = time_features(step_id)
    words_in = text[0]
    pred, kept, words, audio, gu_w = layer_forward(weights, glu_in, sizes, noisy, feats, words_in, flag)
    error = pred - target
    frame_n, chans = pred.shape
    mse = jnp.sum(error * error) / (frame_n * chans)
    d_pred = 2.0 * error / (frame_n * chans)
    audio_vec, pull_audio = jax.vjp(unit_scale, jnp.mean(audio, 0))
    text_vec, pull_text = jax.vjp(unit_scale, jnp.mean(words, 0))
    d_audio_vec, d_text_vec, con = contrast(audio_vec, text_vec, empty, negatives, sizes)
    weight = CON_WEIGHT * (1 - flag).astype(jnp.float32)
    d_audio_extra = pull_audio(d_audio_vec)[0][None, :] / frame_n
    d_words_extra = pull_text(d_text_vec)[0][None, :] / words.shape[0]
    lefts, rights, small = layer_backward(
        weights, gu_w, kept, words_in, d_pred, d_audio_extra, d_words_extra
    )
    loss_local = mse + weight * con
    bucket_local = (jnp.arange(NB, dtype=jnp.int32) == step_id).astype(jnp.float32) * mse
    line = jnp.concatenate([loss_local[None], jnp.zeros((1,), jnp.float32), bucket_local])
    line = jnp.pad(line[None], ((0, 7), (0, LANES - line.shape[0])))
    shares, sums = scatter_grads(lefts, rights, small, masters, line, sizes)
    loss_sum, total_sq, bucket_sums = sums[0], sums[1], sums[2 : 2 + NB]
    grad_norm = jnp.sqrt(total_sq)
    scale = jnp.minimum(1.0, CLIP_NORM / (grad_norm + 1e-06))
    new_weights, new_firsts, new_seconds = ([], [], [])
    for index, (master, first, second, share) in enumerate(zip(masters, firsts, seconds, shares)):
        rate = GAIN_RATE if index == len(masters) - 1 else RATE
        grad = share * scale
        first = BETA_ONE * first + (1.0 - BETA_ONE) * grad
        second = BETA_TWO * second + (1.0 - BETA_TWO) * grad * grad
        fixed_first = first / (1.0 - BETA_ONE**STEP)
        fixed_second = second / (1.0 - BETA_TWO**STEP)
        master = master - rate * (
            fixed_first / (jnp.sqrt(fixed_second) + ADAM_EPS) + DECAY * master
        )
        new_weights.append(master)
        new_firsts.append(first)
        new_seconds.append(second)
    return (
        loss_sum,
        bucket_sums,
        grad_norm,
        new_weights[0],
        new_weights[1],
        new_weights[2],
        new_weights[3],
        new_weights[4],
        new_weights[5],
        new_weights[6],
        new_weights[7],
        new_weights[8],
        new_firsts[0],
        new_firsts[1],
        new_firsts[2],
        new_firsts[3],
        new_firsts[4],
        new_firsts[5],
        new_firsts[6],
        new_firsts[7],
        new_firsts[8],
        new_seconds[0],
        new_seconds[1],
        new_seconds[2],
        new_seconds[3],
        new_seconds[4],
        new_seconds[5],
        new_seconds[6],
        new_seconds[7],
        new_seconds[8],
    )


def solution(mesh):
    sizes = (mesh.shape["dp"], mesh.shape["fsdp"])
    return jax.shard_map(
        functools.partial(body, sizes),
        mesh=mesh,
        in_specs=(
            P(("dp", "fsdp"), None, None),
            P(("dp", "fsdp"), None, None),
            P(("dp", "fsdp"), None, None),
            P(("dp", "fsdp")),
            P(("dp", "fsdp")),
            P(("dp", "fsdp"), None),
            P(None, ("dp", "fsdp")),
            P(("dp", "fsdp"), None),
            P(("dp", "fsdp"), None),
            P(("dp", "fsdp"), None),
            P(("dp", "fsdp"), None),
            P(("dp", "fsdp"), None),
            P(("dp", "fsdp"), None),
            P(("dp", "fsdp"), None),
            P(None, ("dp", "fsdp")),
            P(None, ("dp", "fsdp")),
            P(("dp", "fsdp"), None),
            P(("dp", "fsdp"), None),
            P(("dp", "fsdp"), None),
            P(("dp", "fsdp"), None),
            P(("dp", "fsdp"), None),
            P(("dp", "fsdp"), None),
            P(("dp", "fsdp"), None),
            P(None, ("dp", "fsdp")),
            P(None, ("dp", "fsdp")),
            P(("dp", "fsdp"), None),
            P(("dp", "fsdp"), None),
            P(("dp", "fsdp"), None),
            P(("dp", "fsdp"), None),
            P(("dp", "fsdp"), None),
            P(("dp", "fsdp"), None),
            P(("dp", "fsdp"), None),
            P(None, ("dp", "fsdp")),
        ),
        out_specs=(
            P(),
            P(),
            P(),
            P(None, ("dp", "fsdp")),
            P(("dp", "fsdp"), None),
            P(("dp", "fsdp"), None),
            P(("dp", "fsdp"), None),
            P(("dp", "fsdp"), None),
            P(("dp", "fsdp"), None),
            P(("dp", "fsdp"), None),
            P(("dp", "fsdp"), None),
            P(None, ("dp", "fsdp")),
            P(None, ("dp", "fsdp")),
            P(("dp", "fsdp"), None),
            P(("dp", "fsdp"), None),
            P(("dp", "fsdp"), None),
            P(("dp", "fsdp"), None),
            P(("dp", "fsdp"), None),
            P(("dp", "fsdp"), None),
            P(("dp", "fsdp"), None),
            P(None, ("dp", "fsdp")),
            P(None, ("dp", "fsdp")),
            P(("dp", "fsdp"), None),
            P(("dp", "fsdp"), None),
            P(("dp", "fsdp"), None),
            P(("dp", "fsdp"), None),
            P(("dp", "fsdp"), None),
            P(("dp", "fsdp"), None),
            P(("dp", "fsdp"), None),
            P(None, ("dp", "fsdp")),
        ),
        check_vma=False,
    )
```

```python
import functools
import math

import jax
import jax.numpy as jnp
from jax import lax
from jax.experimental import pallas as pl
from jax.experimental.pallas import tpu as pltpu
from jax.sharding import PartitionSpec as P

AXES = ("dp", "fsdp")
MESH = pl.DeviceIdType.MESH
LANES = 128
COLS = 256
LAGS = (2, 2, 2, 2, 2)
SLOTS = 6
KEPT = 2
PLACES = (("x", "dp", 2), ("core", "dp", 1), ("z1", "fsdp", 4), ("z0", "fsdp", 2), ("y", "fsdp", 1))
ORDERS = (
    ("z1", "z0", "y", "x", "core"),
    ("z1", "z0", "x", "y", "core"),
    ("z1", "z0", "y", "x", "core"),
    ("z1", "z0", "x", "y", "core"),
    ("x", "y", "z1", "z0", "core"),
)
HELD = 20
SPREAD_LAGS = (2, 2, 3, 3, 2)

HD = 64
PAIR = 2 * HD
TF = 256
NB = 8
STEP = 10


EPS_NORM = 1e-05
BETA_ONE = 0.9
BETA_TWO = 0.95
ADAM_EPS = 1e-08
RATE = 0.02
GAIN_RATE = 0.3
DECAY = 0.01
CLIP_NORM = 0.05
CON_WEIGHT = 0.5
INV_TEMP = 50.0
HIGH = lax.Precision.HIGHEST


def matmul(left, right):
    return jnp.dot(left, right, preferred_element_type=jnp.float32)


def matmul_tn(left, right):
    return lax.dot_general(
        left, right, (((0,), (0,)), ((), ())), preferred_element_type=jnp.float32
    )


def matmul_nt(left, right):
    return lax.dot_general(
        left, right, (((1,), (1,)), ((), ())), preferred_element_type=jnp.float32
    )


def layer_norm(x, gain):
    cent = x - jnp.mean(x, axis=-1, keepdims=True)
    var = jnp.mean(cent * cent, axis=-1, keepdims=True)
    return cent * lax.rsqrt(var + EPS_NORM) * gain


def norm_back(x, gain, grad):
    _, pull = jax.vjp(layer_norm, x, gain)
    return pull(grad)


def unit_scale(x):
    return x * lax.rsqrt(jnp.mean(x * x) + EPS_NORM)


def time_features(step_id):
    place = (step_id.astype(jnp.float32) + 0.5) / NB
    half = TF // 2
    freqs = jnp.exp(jnp.arange(half, dtype=jnp.float32) * (math.log(100.0) / half))
    angle = place * freqs
    return jnp.concatenate([jnp.cos(angle), jnp.sin(angle)])


def heads_of(array):
    lane = lax.broadcasted_iota(jnp.int32, array.shape, 1)
    return [jnp.where(lane // HD == head, array, jnp.zeros_like(array)) for head in range(2)]


def attend_kernel(frame_n, query_ref, keys_ref, values_ref, bias_ref, mixed_ref):
    keys = keys_ref[...]
    total = jnp.zeros(mixed_ref.shape, jnp.float32)
    for query, values in zip(heads_of(query_ref[:frame_n]), heads_of(values_ref[...])):
        scores = matmul_nt(query, keys) * HD ** (-0.5) + bias_ref[...]
        rise = jnp.exp(scores - jnp.max(scores, axis=-1, keepdims=True))
        probs = rise * (1.0 / jnp.sum(rise, axis=-1, keepdims=True))
        total += matmul(probs.astype(jnp.bfloat16), values)
    mixed_ref[...] = total.astype(jnp.bfloat16)


def attend(qkv, keep, frame_n):
    seq, width = qkv.shape[0], qkv.shape[1] // 3
    pairs = width // PAIR
    bias = jnp.where(keep, 0.0, -1e30)[None, :]
    return pl.pallas_call(
        functools.partial(attend_kernel, frame_n),
        grid=(pairs,),
        out_shape=jax.ShapeDtypeStruct((frame_n, width), jnp.bfloat16),
        in_specs=[
            pl.BlockSpec((seq, PAIR), lambda p: (0, p)),
            pl.BlockSpec((seq, PAIR), lambda p: (0, pairs + p)),
            pl.BlockSpec((seq, PAIR), lambda p: (0, 2 * pairs + p)),
            pl.BlockSpec((1, seq), lambda p: (0, 0)),
        ],
        out_specs=pl.BlockSpec((frame_n, PAIR), lambda p: (0, p)),
        compiler_params=pltpu.CompilerParams(vmem_limit_bytes=32 * 1024 * 1024),
    )(qkv, qkv, qkv, bias)


def attend_back_kernel(pairs, *refs):
    (query_ref, keys_ref, values_ref, bias_ref, d_after_ref, *refs) = refs
    (out_w_ref, query_w_ref, keys_w_ref, values_w_ref, d_qkv_ref, d_normed_ref) = refs
    pair = pl.program_id(0)
    frame_n = d_after_ref.shape[0]
    bf16 = jnp.bfloat16

    @pl.when(pair == 0)
    def _():
        d_normed_ref[...] = jnp.zeros_like(d_normed_ref)
        d_qkv_ref[...] = jnp.zeros_like(d_qkv_ref)

    keys, values = keys_ref[...], values_ref[...]
    d_mixed = matmul_nt(d_after_ref[...], out_w_ref[...]).astype(bf16)
    parts = zip(heads_of(query_ref[:frame_n]), heads_of(keys), heads_of(d_mixed))
    d_query = jnp.zeros((frame_n, PAIR), jnp.float32)
    d_keys = jnp.zeros(keys.shape, jnp.float32)
    d_values = jnp.zeros(keys.shape, jnp.float32)
    for query, key, d_mix in parts:
        scores = matmul_nt(keys, query) * HD ** (-0.5) + bias_ref[...]
        rise = jnp.exp(scores - jnp.max(scores, axis=0, keepdims=True))
        probs = rise * (1.0 / jnp.sum(rise, axis=0, keepdims=True))
        d_probs = matmul_nt(values, d_mix)
        d_values += matmul(probs.astype(bf16), d_mix)
        weighed = probs * d_probs
        d_scores = (weighed - probs * jnp.sum(weighed, axis=0, keepdims=True)).astype(bf16)
        d_keys += matmul(d_scores, query)
        d_query += matmul_tn(d_scores, key)
    d_query = (d_query * HD ** (-0.5)).astype(bf16)
    d_keys = (d_keys * HD ** (-0.5)).astype(bf16)
    d_values = d_values.astype(bf16)

    def lanes(part):
        return pl.ds(pl.multiple_of((part * pairs + pair) * PAIR, PAIR), PAIR)

    d_qkv_ref[:frame_n, lanes(0)] = d_query
    d_qkv_ref[:, lanes(1)] = d_keys
    d_qkv_ref[:, lanes(2)] = d_values
    d_normed_ref[:frame_n] += matmul_nt(d_query, query_w_ref[...])
    d_normed_ref[...] += matmul_nt(d_keys, keys_w_ref[...]) + matmul_nt(d_values, values_w_ref[...])


def attend_back(qkv, keep, d_after, qkv_w, out_w, out_place):
    (seq, width), frame_n = (qkv.shape[0], d_after.shape[1]), d_after.shape[0]
    pairs = width // PAIR
    bias = jnp.where(keep, 0.0, -1e30)[:, None]

    def piece(rows, part):
        return pl.BlockSpec((rows, PAIR), lambda p: (0, part * pairs + p))

    return pl.pallas_call(
        functools.partial(attend_back_kernel, pairs),
        grid=(pairs,),
        out_shape=[
            jax.ShapeDtypeStruct((seq, 3 * width), jnp.bfloat16),
            jax.ShapeDtypeStruct((seq, width), jnp.float32),
        ],
        in_specs=[
            piece(seq, 0),
            piece(seq, 1),
            piece(seq, 2),
            pl.BlockSpec((seq, 1), lambda p: (0, 0)),
            pl.BlockSpec((frame_n, width), lambda p: (0, 0)),
            pl.BlockSpec((PAIR, width), lambda p: (p, out_place)),
            piece(width, 0),
            piece(width, 1),
            piece(width, 2),
        ],
        out_specs=[
            pl.BlockSpec((seq, 3 * width), lambda p: (0, 0)),
            pl.BlockSpec((seq, width), lambda p: (0, 0)),
        ],
        compiler_params=pltpu.CompilerParams(vmem_limit_bytes=48 * 1024 * 1024),
    )(qkv, qkv, qkv, bias, d_after, out_w, qkv_w, qkv_w, qkv_w)


def gated_back_kernel(d_final_ref, down_ref, gate_ref, up_ref, gate_w_ref, up_w_ref, *outs):
    (d_gate_ref, d_up_ref, inner_ref, d_normed_ref) = outs
    bf16 = jnp.bfloat16
    d_inner = matmul_nt(d_final_ref[...], down_ref[...])
    gate, up = gate_ref[...].astype(jnp.float32), up_ref[...].astype(jnp.float32)
    sig = jax.nn.sigmoid(gate)
    held = gate * sig
    inner_ref[...] = (held * up).astype(bf16).T
    d_gate = (d_inner * up * (sig * (1.0 + gate * (1.0 - sig)))).astype(bf16)
    d_up = (d_inner * held).astype(bf16)
    d_gate_ref[...] = d_gate
    d_up_ref[...] = d_up
    both = matmul_nt(d_gate, gate_w_ref[...]) + matmul_nt(d_up, up_w_ref[...])

    @pl.when(pl.program_id(0) == 0)
    def _():
        d_normed_ref[...] = both

    @pl.when(pl.program_id(0) > 0)
    def _():
        d_normed_ref[...] += both


def gated_back(d_final, gate_up, down_w, gu_w):
    frame_n, width = d_final.shape
    units = down_w.shape[0]
    block = min(1024, units)
    steps = units // block
    part = pl.BlockSpec((frame_n, block), lambda u: (0, u))
    return pl.pallas_call(
        gated_back_kernel,
        grid=(steps,),
        out_shape=[
            jax.ShapeDtypeStruct((frame_n, units), jnp.bfloat16),
            jax.ShapeDtypeStruct((frame_n, units), jnp.bfloat16),
            jax.ShapeDtypeStruct((units, frame_n), jnp.bfloat16),
            jax.ShapeDtypeStruct((frame_n, width), jnp.float32),
        ],
        in_specs=[
            pl.BlockSpec((frame_n, width), lambda u: (0, 0)),
            pl.BlockSpec((block, width), lambda u: (u, 0)),
            part,
            pl.BlockSpec((frame_n, block), lambda u: (0, steps + u)),
            pl.BlockSpec((width, block), lambda u: (0, u)),
            pl.BlockSpec((width, block), lambda u: (0, steps + u)),
        ],
        out_specs=[
            part,
            part,
            pl.BlockSpec((block, frame_n), lambda u: (u, 0)),
            pl.BlockSpec((frame_n, width), lambda u: (0, 0)),
        ],
        compiler_params=pltpu.CompilerParams(vmem_limit_bytes=48 * 1024 * 1024),
    )(d_final, down_w, gate_up, gate_up, gu_w, gu_w)


def layer_forward(weights, gu_share, sizes, noisy, feats, words_in, flag):
    lat_w, time_w, text_w, packed, down_w, lout_w, gains = weights
    width = lat_w.shape[1]
    qkv_w, out_w = packed[:, : 3 * width], packed[:, 3 * width : 4 * width]
    gains = gains.astype(jnp.float32)
    frame_n = noisy.shape[0]
    noisy_b = noisy.astype(jnp.bfloat16)
    feats_b = feats.astype(jnp.bfloat16)[None]
    frames = matmul(noisy_b, lat_w) + matmul(feats_b, time_w)
    words = matmul(words_in, text_w)
    hidden = jnp.concatenate([frames, words], 0)
    seq = hidden.shape[0]
    normed_b = layer_norm(hidden, gains[0]).astype(jnp.bfloat16)
    qkv = matmul(normed_b, qkv_w).astype(jnp.bfloat16)
    keep = (jnp.arange(seq) < frame_n) | (flag == 0)
    mixed_b = attend(qkv, keep, frame_n)
    after = frames + matmul(mixed_b, out_w)
    normed2_b = layer_norm(after, gains[1]).astype(jnp.bfloat16)
    gu_w, gate_up = up_project(normed2_b, gu_share, sizes)
    ffw = gate_up.shape[1] // 2
    gate = gate_up[:, :ffw].astype(jnp.float32)
    up = gate_up[:, ffw:].astype(jnp.float32)
    inner_b = (jax.nn.silu(gate) * up).astype(jnp.bfloat16)
    final = after + matmul(inner_b, down_w)
    audio = final
    out_b = layer_norm(audio, gains[2]).astype(jnp.bfloat16)
    pred = matmul(out_b, lout_w)
    kept = (
        noisy_b,
        feats,
        hidden,
        normed_b,
        qkv,
        keep,
        mixed_b,
        after,
        normed2_b,
        gate_up,
        inner_b,
        audio,
        out_b,
    )
    return (pred, kept, words, audio, gu_w)


def layer_backward(weights, gu_w, kept, words_in, d_pred, d_audio_extra, d_words_extra):
    _, _, _, packed, down_w, lout_w, gains = weights
    gains = gains.astype(jnp.float32)
    (
        noisy_b,
        feats,
        hidden,
        normed_b,
        qkv,
        keep,
        mixed_b,
        after,
        normed2_b,
        gate_up,
        inner_b,
        audio,
        out_b,
    ) = kept
    frame_n = audio.shape[0]
    d_pred_b = d_pred.astype(jnp.bfloat16)
    g_lout = matmul_tn(out_b, d_pred_b)
    d_audio, g_gain2 = norm_back(audio, gains[2], matmul_nt(d_pred_b, lout_w))
    d_final = d_audio + d_audio_extra
    d_final_b = d_final.astype(jnp.bfloat16)
    d_gate_b, d_up_b, inner_t, d_normed2 = gated_back(d_final_b, gate_up, down_w, gu_w)
    d_after_n, g_gain1 = norm_back(after, gains[1], d_normed2)
    d_after = d_final + d_after_n
    d_after_b = d_after.astype(jnp.bfloat16)
    d_qkv_b, d_normed = attend_back(qkv, keep, d_after_b, packed, packed, 3)
    d_hidden_n, g_gain0 = norm_back(hidden, gains[0], d_normed)
    d_frames_b = (d_after + d_hidden_n[:frame_n]).astype(jnp.bfloat16)
    d_words_b = (d_hidden_n[frame_n:] + d_words_extra).astype(jnp.bfloat16)
    g_lat = matmul_tn(d_frames_b, noisy_b)
    column = jnp.sum(d_frames_b.astype(jnp.float32), 0)
    feats_low = lax.reduce_precision(feats, 8, 7)
    g_text = matmul_tn(words_in, d_words_b)
    g_gains = jnp.stack([g_gain0, g_gain1, g_gain2])
    lefts = (normed2_b.T, inner_t, mixed_b.T, normed_b.T)
    rights = (d_gate_b, d_up_b, d_final_b, d_after_b, d_qkv_b)
    return (lefts, rights, (g_lat, column, feats_low, g_text, g_lout, g_gains))


def mine(axis, bit):
    return lax.rem(lax.axis_index(axis) // bit, 2)


def partner(axis, bit):
    return {axis: lax.axis_index(axis) + bit * (1 - 2 * mine(axis, bit))}


def greet(steps):
    barrier = pltpu.get_barrier_semaphore()
    for axis, bit in steps:
        pl.semaphore_signal(barrier, inc=1, device_id=partner(axis, bit), device_id_type=MESH)
    pl.semaphore_wait(barrier, len(steps))


def gather_kernel(sizes, block_ref, all_ref, send_sem, recv_sem):
    dp_size, fsdp_size = sizes
    dp, fsdp = lax.axis_index("dp"), lax.axis_index("fsdp")
    rounds = (("fsdp", fsdp, fsdp_size, 1), ("dp", dp, dp_size, fsdp_size))
    barrier = pltpu.get_barrier_semaphore()
    for axis, place, size, _ in rounds:
        for hop in range(1, size):
            peer = {axis: lax.rem(place + hop, size)}
            pl.semaphore_signal(barrier, inc=1, device_id=peer, device_id_type=MESH)
    pl.semaphore_wait(barrier, dp_size + fsdp_size - 2)
    all_ref[pl.ds(dp * fsdp_size + fsdp, 1)] = block_ref[...][None]
    first = 0
    for axis, place, size, span in rounds:

        def copy(hop, owner):
            start = dp * fsdp_size + owner if axis == "fsdp" else owner * fsdp_size
            held = all_ref.at[pl.ds(start, span)]
            return pltpu.make_async_remote_copy(
                src_ref=held,
                dst_ref=held,
                send_sem=send_sem.at[first + hop - 1],
                recv_sem=recv_sem.at[first + hop - 1],
                device_id={axis: lax.rem(place + hop, size)},
                device_id_type=MESH,
            )

        for hop in range(1, size):
            copy(hop, place).start()
        for hop in range(1, size):
            copy(hop, lax.rem(place + size - hop, size)).wait_recv()
            copy(hop, place).wait_send()
        first += size - 1


def gather_everywhere(block, sizes):
    count = sizes[0] + sizes[1] - 2
    return pl.pallas_call(
        functools.partial(gather_kernel, sizes),
        out_shape=jax.ShapeDtypeStruct((sizes[0] * sizes[1],) + block.shape, block.dtype),
        in_specs=[pl.BlockSpec(memory_space=pltpu.VMEM)],
        out_specs=pl.BlockSpec(memory_space=pltpu.VMEM),
        scratch_shapes=[pltpu.SemaphoreType.DMA((count,)), pltpu.SemaphoreType.DMA((count,))],
        compiler_params=pltpu.CompilerParams(collective_id=0, has_side_effects=True),
    )(block)


def scatter_kernel(plan, *refs):
    rows, folds = plan["rows"], plan["folds"]
    (xt_gu, xt_down, xt_out, xt_qkv, *rest) = refs
    (dy_gate, dy_up, dy_down, dy_out, dy_qkv, text, time, small, line, *rest) = rest
    (o_gu, o_down, o_out, o_qkv, o_text, o_time, o_small, o_line, *rest) = rest
    (xs, xq, dya, dyq, ss, rr, kk, final, squares, part, came, *rest) = rest
    (load_sem, dy_sem, misc_sem, send_sem, recv_sem, out_sem, line_sem) = rest
    wide = [d.shape[1] // COLS for d in (dy_gate, dy_up, dy_down, dy_out, dy_qkv)]
    wide[2] *= folds
    wide += [text.shape[1] // (2 * COLS), time.shape[1] // COLS, small.shape[1] // COLS]
    ends = [sum(wide[: i + 1]) for i in range(len(wide))]
    starts = [0] + ends[:-1]
    total = ends[-1]
    first_q, first_misc = starts[4], starts[5]
    per_fold = wide[2] // folds
    stages = (("dp", 1), ("dp", 2), ("fsdp", 1), ("fsdp", 2), ("fsdp", 4))
    after = [sum(LAGS[:k]) for k in range(6)]
    greet(stages)

    dp, fsdp = lax.axis_index("dp"), lax.axis_index("fsdp")
    core, x = lax.rem(dp, 2), dp // 2
    y, z0, z1 = lax.rem(fsdp, 2), lax.rem(fsdp // 2, 2), fsdp // 4

    def owner(block):
        def bit(own, weight):
            same = lax.rem(block // weight, 2)
            return own + (1 - same) * (1 - 2 * own)

        where = bit(x, 8) * 2 + bit(core, 16)
        return where * 8 + bit(z1, 1) * 4 + bit(z0, 2) * 2 + bit(y, 4)

    def load(source, fold, dest, index, reach):
        def one(block, carry):
            first = pl.multiple_of(owner(block) * (reach * rows) + fold * rows, 16)
            pltpu.make_async_copy(
                source.at[pl.ds(first, rows)], dest.at[block], load_sem.at[index]
            ).start()
            return carry

        lax.fori_loop(0, 32, one, 0)

    load(xt_gu, 0, xs.at[0], 0, 1)
    for fold in range(folds):
        load(xt_down, fold, xs.at[1 + fold], 1 + fold, folds)
    load(xt_out, 0, xs.at[1 + folds], 1 + folds, 1)
    load(xt_qkv, 0, xq, 2 + folds, 1)

    def columns(tile):
        return pl.ds(pl.multiple_of(tile * COLS, COLS), COLS)

    def within(tile, low, high):
        return (tile >= low) & (tile < high)

    def fetch(tile):
        slot = lax.rem(tile, 2)
        for index, source in enumerate((dy_gate, dy_up, dy_down, dy_out, dy_qkv)):
            dest = dya if index < 4 else dyq

            @pl.when(within(tile, starts[index], ends[index]))
            def _(index=index, source=source, dest=dest):
                place = lax.rem(tile - starts[index], source.shape[1] // COLS)
                pltpu.make_async_copy(
                    source.at[:, columns(place)], dest.at[slot], dy_sem.at[slot]
                ).start()

    def product(left, right, half, keep):
        def some(step, carry):
            lhs = left[pl.ds(half * 16 + step * 4, 4)]
            out = jnp.dot(
                lhs.reshape(4 * rows, lhs.shape[-1]), right[...], preferred_element_type=jnp.float32
            )
            keep[pl.ds(pl.multiple_of(step * 4, 4), 4)] = out.reshape(4, rows, COLS)
            return carry

        lax.fori_loop(0, 4, some, 0)

    def copy(stage, parity, tile):
        axis, bit = stages[stage]
        if parity and stage in (1, 2):
            axis, bit = stages[3 - stage]
        slot = lax.rem(tile, SLOTS)
        return pltpu.make_async_remote_copy(
            src_ref=ss[stage].at[slot],
            dst_ref=rr[stage].at[slot],
            send_sem=send_sem.at[stage, slot],
            recv_sem=recv_sem.at[stage, slot],
            device_id=partner(axis, bit),
            device_id_type=MESH,
        )

    def out_copies(tile):
        slot = lax.rem(tile, 2)
        half = rows // 2
        for index, dest in enumerate(
            (o_gu, o_gu, o_down, o_out, o_qkv, o_text, o_time, o_small)
        ):

            @pl.when(within(tile, starts[index], ends[index]))
            def _(index=index, dest=dest):
                place, row = tile - starts[index], 0
                if index == 1:
                    place = place + wide[0]
                if index == 2:
                    row = pl.multiple_of((place // per_fold) * rows, 8)
                    place = lax.rem(place, per_fold)
                if index == 5:
                    for side in range(2):
                        pltpu.make_async_copy(
                            final.at[slot, pl.ds(side * half, half)],
                            dest.at[:, columns(side * wide[5] + place)],
                            out_sem.at[slot],
                        ).start()
                else:
                    pltpu.make_async_copy(
                        final.at[slot], dest.at[pl.ds(row, rows), columns(place)], out_sem.at[slot]
                    ).start()

    def wait_out(tile):
        slot = lax.rem(tile, 2)
        pltpu.make_async_copy(final.at[slot], o_gu.at[:, columns(0)], out_sem.at[slot]).wait()

    def freed(stage, parity, tile):
        @pl.when((tile >= SLOTS) & (tile < total + SLOTS) & (lax.rem(tile, 2) == parity))
        def _():
            copy(stage, parity, tile - SLOTS).wait_send()

    def make(tile):
        freed(0, 0, tile)
        freed(0, 1, tile)

        @pl.when(tile < total)
        def _():
            side = lax.rem(tile, 2)
            send, keep = ss[0].at[lax.rem(tile, SLOTS)], kk[0].at[lax.rem(tile, KEPT)]

            @pl.when(tile + 1 < first_misc)
            def _():
                fetch(tile + 1)

            @pl.when(tile < first_q)
            def _():
                pltpu.make_async_copy(dy_gate.at[:, columns(0)], dya.at[side], dy_sem.at[side]).wait()
                fold = (tile - starts[2]) // per_fold
                which = jnp.where(tile >= ends[2], 1 + folds, 1 + fold)
                left = xs.at[jnp.where(tile < starts[2], 0, which)]
                product(left, dya.at[side], 0, send)
                copy(0, 0, tile).start()
                product(left, dya.at[side], 1, keep)

            @pl.when(within(tile, first_q, first_misc))
            def _():
                pltpu.make_async_copy(dy_qkv.at[:, columns(0)], dyq.at[side], dy_sem.at[side]).wait()
                product(xq, dyq.at[side], 0, send)
                copy(0, 0, tile).start()
                product(xq, dyq.at[side], 1, keep)

            @pl.when(tile >= first_misc)
            def _():
                def one(block, carry):
                    for index, dest in enumerate((send, keep)):
                        who = owner(block + 16 * index)

                        def bring(source, row, place, low, count, dest=dest, index=index):
                            pltpu.make_async_copy(
                                source.at[pl.ds(pl.multiple_of(row, 8), count), columns(place)],
                                dest.at[block, pl.ds(low, count)],
                                misc_sem.at[index],
                            ).start()

                        @pl.when(tile < ends[5])
                        def _():
                            half = rows // 2
                            for part_of in range(2):
                                place = part_of * wide[5] + tile - starts[5]
                                bring(text, who * half, place, part_of * half, half)

                        @pl.when(within(tile, starts[6], ends[6]))
                        def _():
                            bring(time, who * rows, tile - starts[6], 0, rows)

                        @pl.when(tile >= starts[7])
                        def _():
                            bring(small, who * rows, tile - starts[7], 0, rows)

                    return carry

                lax.fori_loop(0, 16, one, 0)
                pltpu.make_async_copy(send, send, misc_sem.at[0]).wait()
                copy(0, 0, tile).start()
                pltpu.make_async_copy(keep, keep, misc_sem.at[1]).wait()

    def pass_on(stage, parity, tile):
        freed(stage, parity, tile)

        @pl.when(within(tile, 0, total) & (lax.rem(tile, 2) == parity))
        def _():
            slot = lax.rem(tile, SLOTS)
            copy(stage - 1, parity, tile).wait_recv()
            came_in, held = rr[stage - 1].at[slot], kk[stage - 1].at[lax.rem(tile, KEPT)]
            send, keep = ss[stage].at[slot], kk[stage].at[lax.rem(tile, KEPT)]
            half = 32 >> (stage + 1)
            group = half // 2 if (stage == 1 and parity) else half

            def first(block, carry):
                low = block + (block // group) * group
                send[block] = (held[low] + came_in[low].astype(jnp.float32)).astype(send.dtype)
                return carry

            def second(block, carry):
                high = block + (block // group) * group + group
                keep[block] = held[high] + came_in[high].astype(jnp.float32)
                return carry

            lax.fori_loop(0, half, first, 0)
            copy(stage, parity, tile).start()
            lax.fori_loop(0, half, second, 0)

    def finish(tile):
        @pl.when(within(tile, 2, total + 2))
        def _():
            wait_out(tile)

        @pl.when(within(tile, 0, total))
        def _():
            copy(4, 0, tile).wait_recv()
            held, came_in = kk[4].at[lax.rem(tile, KEPT)], rr[4].at[lax.rem(tile, SLOTS)]
            sums = held[0] + came_in[0].astype(jnp.float32)
            final[lax.rem(tile, 2)] = sums
            squares[...] += sums * sums
            out_copies(tile)

    squares[...] = jnp.zeros_like(squares)
    fetch(0)
    for index in range(3 + folds):
        dest = xq if index == 2 + folds else xs.at[index]
        pltpu.make_async_copy(dest, dest, load_sem.at[index]).wait()

    def step(now, carry):
        finish(now - after[5])
        for stage in (4, 3, 2, 1):
            pass_on(stage, 0, now - after[stage])
            pass_on(stage, 1, now - after[stage])
        make(now)
        return carry

    lax.fori_loop(0, total + max(after[5] + 2, after[4] + SLOTS), step, 0)

    row = lax.broadcasted_iota(jnp.int32, line.shape, 0)
    lane = lax.broadcasted_iota(jnp.int32, line.shape, 1)
    part[0] = line[...] + jnp.where((row == 0) & (lane == 1), jnp.sum(squares[...]), 0.0)
    for index, (axis, bit) in enumerate(stages):
        swap = pltpu.make_async_remote_copy(
            src_ref=part.at[index],
            dst_ref=came.at[index],
            send_sem=line_sem.at[0, index],
            recv_sem=line_sem.at[1, index],
            device_id=partner(axis, bit),
            device_id_type=MESH,
        )
        swap.start()
        swap.wait()
        part[index + 1] = part[index] + came[index]
    o_line[...] = part[len(stages)]


def scatter_sums(xts, dys, misc, line):
    xt_gu, xt_down, xt_out, xt_qkv = xts
    dy_gate, dy_up, dy_down, dy_out, dy_qkv = dys
    text, time, small = misc
    rows = xt_gu.shape[0] // 32
    folds = xt_down.shape[0] // xt_gu.shape[0]
    plan = {"rows": rows, "folds": folds}
    sizes = [16 >> stage for stage in range(5)]
    f32, bf16 = jnp.float32, jnp.bfloat16
    link_types = (f32, bf16, bf16, f32, f32)
    scratch = [
        pltpu.VMEM((2 + folds, 32, rows, xt_gu.shape[1]), bf16),
        pltpu.VMEM((32, rows, xt_qkv.shape[1]), bf16),
        pltpu.VMEM((2, xt_gu.shape[1], COLS), bf16),
        pltpu.VMEM((2, xt_qkv.shape[1], COLS), bf16),
        [pltpu.VMEM((SLOTS, n, rows, COLS), t) for n, t in zip(sizes, link_types)],
        [pltpu.VMEM((SLOTS, n, rows, COLS), t) for n, t in zip(sizes, link_types)],
        [pltpu.VMEM((KEPT, n, rows, COLS), f32) for n in sizes],
        pltpu.VMEM((2, rows, COLS), f32),
        pltpu.VMEM((rows, COLS), f32),
        pltpu.VMEM((6,) + line.shape, f32),
        pltpu.VMEM((5,) + line.shape, f32),
        pltpu.SemaphoreType.DMA((3 + folds,)),
        pltpu.SemaphoreType.DMA((2,)),
        pltpu.SemaphoreType.DMA((2,)),
        pltpu.SemaphoreType.DMA((5, SLOTS)),
        pltpu.SemaphoreType.DMA((5, SLOTS)),
        pltpu.SemaphoreType.DMA((2,)),
        pltpu.SemaphoreType.DMA((2, 5)),
    ]

    def out(height, width):
        return jax.ShapeDtypeStruct((height, width), f32)

    width = dy_down.shape[1]
    outs = [
        out(rows, dy_gate.shape[1] + dy_up.shape[1]),
        out(rows * folds, width),
        out(rows, width),
        out(rows, dy_qkv.shape[1]),
        out(rows // 2, text.shape[1]),
        out(rows, time.shape[1]),
        out(rows, small.shape[1]),
        jax.ShapeDtypeStruct(line.shape, f32),
    ]
    in_hbm = pl.BlockSpec(memory_space=pl.ANY)
    in_vmem = pl.BlockSpec(memory_space=pltpu.VMEM)
    return pl.pallas_call(
        functools.partial(scatter_kernel, plan),
        out_shape=outs,
        in_specs=[in_hbm] * 12 + [in_vmem],
        out_specs=[in_hbm] * 7 + [in_vmem],
        scratch_shapes=scratch,
        compiler_params=pltpu.CompilerParams(
            collective_id=2, has_side_effects=True, vmem_limit_bytes=56 * 1024 * 1024
        ),
    )(*xts, *dys, *misc, line)


def spread_kernel(total, multiply, *refs):
    if multiply:
        (share, left, full, product, whole, result, send_sem, recv_sem, full_sem, out_sem) = refs
    else:
        (share, early, full, late, whole, send_sem, recv_sem, full_sem, late_sem) = refs
        hand_on = pltpu.make_async_copy(early, late, late_sem)
        hand_on.start()
    greet([(axis, bit) for _, axis, bit in PLACES])
    after = [sum(SPREAD_LAGS[:k]) for k in range(6)]
    mine_at = {name: mine(axis, bit) for name, axis, bit in PLACES}
    links_of = {name: (axis, bit) for name, axis, bit in PLACES}

    def columns(tile):
        return pl.ds(pl.multiple_of(tile * COLS, COLS), COLS)

    def held(order, stage, slot):
        done = order[:stage]
        where = tuple(slice(None) if n in done else mine_at[n] for n, _, _ in PLACES)
        return whole.at[(slot,) + where]

    def copy(order, stage, tile):
        slot = lax.rem(tile, HELD)
        group = held(order, stage, slot)
        return pltpu.make_async_remote_copy(
            src_ref=group,
            dst_ref=group,
            send_sem=send_sem.at[stage, slot],
            recv_sem=recv_sem.at[stage, slot],
            device_id=partner(*links_of[order[stage]]),
            device_id_type=MESH,
        )

    def each_order(tile, act):
        for kind, order in enumerate(ORDERS):

            @pl.when((tile >= 0) & (tile < total) & (lax.rem(tile, len(ORDERS)) == kind))
            def _(order=order):
                act(order)

    def write(tile):
        slot = lax.rem(tile, HELD)
        return pltpu.make_async_copy(
            whole.at[slot], full.at[:, :, :, :, :, :, columns(tile)], full_sem.at[lax.rem(tile, 2)]
        )

    def give(tile):
        slot = lax.rem(tile, 2)
        return pltpu.make_async_copy(
            result.at[slot], product.at[:, columns(tile)], out_sem.at[slot]
        )

    def step(now, carry):
        last = now - after[5]

        @pl.when((last >= 1) & (last <= total))
        def _():
            write(last - 1).wait()

        def end(order):
            for stage in range(5):
                copy(order, stage, last).wait_send()
            copy(order, 4, last).wait_recv()

        each_order(last, end)

        @pl.when((last >= 0) & (last < total))
        def _():
            write(last).start()
            if multiply:

                @pl.when(last >= 2)
                def _():
                    give(last - 2).wait()

                tile = whole[lax.rem(last, HELD)]
                result[lax.rem(last, 2)] = jnp.dot(
                    left[...],
                    tile.reshape(left.shape[1], COLS),
                    preferred_element_type=jnp.float32,
                ).astype(result.dtype)
                give(last).start()

        for stage in (4, 3, 2, 1):
            tile = now - after[stage]

            def onward(order, stage=stage, tile=tile):
                copy(order, stage - 1, tile).wait_recv()
                copy(order, stage, tile).start()

            each_order(tile, onward)

        @pl.when(now < total)
        def _():
            place = tuple(mine_at[n] for n, _, _ in PLACES)
            whole[(lax.rem(now, HELD),) + place] = share[:, columns(now)].astype(whole.dtype)

        each_order(now, lambda order: copy(order, 0, now).start())
        return carry

    lax.fori_loop(0, total + after[5] + 1, step, 0)
    if multiply:
        for tile in range(max(total - 2, 0), total):
            give(tile).wait()
    else:
        hand_on.wait()


def spread(share, left, early, identity):
    rows, width = share.shape
    total = width // COLS
    bf16 = jnp.bfloat16
    places = (2,) * 5
    out_shape = [jax.ShapeDtypeStruct(places + (rows, width), bf16)]
    scratch = [pltpu.VMEM((HELD,) + places + (rows, COLS), bf16)]
    sems = [pltpu.SemaphoreType.DMA((5, HELD))] * 2 + [pltpu.SemaphoreType.DMA((2,))]
    in_hbm = pl.BlockSpec(memory_space=pl.ANY)
    in_specs = [pl.BlockSpec(memory_space=pltpu.VMEM)] * 2
    if left is None:
        args = [share, early]
        in_specs[1] = in_hbm
        out_shape.append(jax.ShapeDtypeStruct(early.shape, early.dtype))
        sems.append(pltpu.SemaphoreType.DMA)
    else:
        args = [share, left]
        out_shape.append(jax.ShapeDtypeStruct((left.shape[0], width), bf16))
        scratch.append(pltpu.VMEM((2, left.shape[0], COLS), bf16))
        sems.append(pltpu.SemaphoreType.DMA((2,)))
    results = pl.pallas_call(
        functools.partial(spread_kernel, total, left is not None),
        out_shape=out_shape,
        in_specs=in_specs,
        out_specs=[in_hbm] * 2,
        scratch_shapes=scratch + sems,
        compiler_params=pltpu.CompilerParams(
            collective_id=identity, has_side_effects=True, vmem_limit_bytes=40 * 1024 * 1024
        ),
    )(*args)
    return [results[0].reshape(32 * rows, width)] + list(results[1:])


def fold(share, rows):
    return share.reshape(rows, share.size // rows)


def unstack(stacked, few):
    pieces = stacked.shape[0] // few
    return stacked.reshape(pieces, few, -1).swapaxes(0, 1).reshape(few, -1)


def by_tiles(sizes, rows):
    return sizes == (4, 8) and rows % 16 == 0


def whole_rows(share):
    return lax.all_gather(share.astype(jnp.bfloat16), AXES, axis=0, tiled=True)


def gather_weights(masters, sizes):
    lat, time, text, qkv, out, _, down, lout, gains = masters
    rows, width = out.shape
    gains_t = jnp.pad(gains.T, ((0, 0), (0, LANES - gains.shape[0])))
    pieces = [qkv, out, fold(text, rows), fold(time, rows), lat.T, lout, gains_t]
    packed = jnp.concatenate(pieces, 1).astype(jnp.bfloat16)
    low_down = down.astype(jnp.bfloat16)
    if by_tiles(sizes, rows):
        gathered, low_down = spread(packed, None, low_down, 3)
    else:
        gathered = whole_rows(packed)
    full, start = [], 0
    for piece in pieces:
        full.append(gathered[:, start : start + piece.shape[1]])
        start += piece.shape[1]
    return (
        full[4].T,
        full[3].reshape(-1, width),
        full[2].reshape(-1, width),
        gathered,
        whole_rows(low_down),
        full[5],
        full[6][:, : gains.shape[0]].T,
    )


def up_project(normed, share, sizes):
    if by_tiles(sizes, share.shape[0]):
        return spread(share, normed, None, 4)
    weight = whole_rows(share)
    return (weight, matmul(normed, weight).astype(jnp.bfloat16))


def scatter_grads(lefts, rights, small, masters, line, sizes):
    lat, column, feats, text, lout, gains = small
    rows = masters[3].shape[0]
    few = masters[1].shape[0]
    pieces = rows // few
    time = (
        feats.reshape(-1, 1, few, 1) * column.reshape(1, pieces, 1, column.shape[0] // pieces)
    ).reshape(-1, column.shape[0] // pieces)
    gains_t = jnp.pad(gains.T, ((0, 0), (0, LANES - gains.shape[0])))
    packed = jnp.concatenate([lat, lout, gains_t], 1)
    chans = lat.shape[1]
    if by_tiles(sizes, rows):
        gu, down, out, qkv, g_text, g_time, g_small, line = scatter_sums(
            lefts, rights, [text, time, packed], line
        )
    else:
        d_gate, d_up, d_final, d_after, d_qkv = rights
        d_gu = jnp.concatenate([d_gate, d_up], 1)
        grads = [matmul(x, d) for x, d in zip(lefts, (d_gu, d_final, d_after, d_qkv))]
        gu, down, out, qkv, g_text, g_time, g_small = sums = [
            lax.psum_scatter(g, AXES, scatter_dimension=0, tiled=True)
            for g in grads + [text, time, packed]
        ]
        squares = sum(jnp.sum(g * g) for g in sums)
        line = lax.psum(line.at[0, 1].set(squares), AXES)
    shares = (
        g_small[:, :chans].T,
        unstack(g_time, few),
        g_text,
        qkv,
        out,
        gu,
        down,
        g_small[:, chans : 2 * chans],
        g_small[:, 2 * chans : 2 * chans + gains.shape[0]].T,
    )
    return (shares, line[0])


def contrast(audio_vec, text_vec, empty, negatives, sizes):
    width = audio_vec.shape[0]
    lines = width // LANES
    me = lax.axis_index(AXES)
    facts = jnp.concatenate([empty, me[None], negatives[0]]).astype(jnp.float32)
    block = jnp.concatenate(
        [
            audio_vec.reshape(lines, LANES),
            lax.reduce_precision(text_vec, 8, 7).reshape(lines, LANES),
            jnp.pad(facts, (0, LANES - facts.shape[0]))[None],
        ]
    )
    block = jnp.pad(block, ((0, -block.shape[0] % 8), (0, 0)))
    everyone = gather_everywhere(block, sizes)
    clips = everyone.shape[0]
    audios = everyone[:, :lines].reshape(clips, width)
    texts = everyone[:, lines : 2 * lines].reshape(clips, width)
    flags = everyone[:, 2 * lines, 0]
    picks = everyone[:, 2 * lines, 1 : 2 + negatives.shape[1]].astype(jnp.int32)
    coeff = INV_TEMP / width
    places = jnp.arange(clips, dtype=jnp.int32)
    onehot = (picks[:, :, None] == places[None, None, :]).astype(jnp.float32)
    cross = coeff * jnp.einsum("cd,td->ct", audios, texts, precision=HIGH)
    sims = jnp.sum(onehot * cross[:, None, :], axis=2)
    total = jax.nn.logsumexp(sims, axis=1, keepdims=True)
    weights = CON_WEIGHT * (1.0 - flags)[:, None]
    first_pick = (jnp.arange(sims.shape[1]) == 0).astype(jnp.float32)[None, :]
    d_sims = weights * (jnp.exp(sims - total) - first_pick)
    d_cross = coeff * jnp.sum(onehot * d_sims[:, :, None], axis=1)
    is_me = (places == me).astype(jnp.float32)
    d_audio_vec = jnp.dot(jnp.sum(d_cross * is_me[:, None], axis=0), texts, precision=HIGH)
    d_text_vec = jnp.dot(jnp.sum(d_cross * is_me[None, :], axis=1), audios, precision=HIGH)
    con = jnp.sum((total[:, 0] - sims[:, 0]) * is_me)
    return (d_audio_vec, d_text_vec, con)


def body(
    sizes,
    latent,
    noise,
    text,
    steps,
    empty,
    negatives,
    latent_in,
    time_proj,
    text_proj,
    attn_qkv,
    attn_out,
    glu_in,
    glu_out,
    latent_out,
    norm_gains,
    first_latent_in,
    first_time_proj,
    first_text_proj,
    first_attn_qkv,
    first_attn_out,
    first_glu_in,
    first_glu_out,
    first_latent_out,
    first_norm_gains,
    second_latent_in,
    second_time_proj,
    second_text_proj,
    second_attn_qkv,
    second_attn_out,
    second_glu_in,
    second_glu_out,
    second_latent_out,
    second_norm_gains,
):
    masters = (
        latent_in,
        time_proj,
        text_proj,
        attn_qkv,
        attn_out,
        glu_in,
        glu_out,
        latent_out,
        norm_gains,
    )
    firsts = (
        first_latent_in,
        first_time_proj,
        first_text_proj,
        first_attn_qkv,
        first_attn_out,
        first_glu_in,
        first_glu_out,
        first_latent_out,
        first_norm_gains,
    )
    seconds = (
        second_latent_in,
        second_time_proj,
        second_text_proj,
        second_attn_qkv,
        second_attn_out,
        second_glu_in,
        second_glu_out,
        second_latent_out,
        second_norm_gains,
    )
    weights = gather_weights(masters, sizes)
    step_id = steps[0]
    flag = empty[0]
    place = (step_id.astype(jnp.float32) + 0.5) / NB
    alpha = jnp.cos(0.5 * jnp.pi * place)
    sigma = jnp.sin(0.5 * jnp.pi * place)
    clean = latent[0]
    fresh = noise[0]
    noisy = alpha * clean + sigma * fresh
    target = alpha * fresh - sigma * clean
    feats = time_features(step_id)
    words_in = text[0]
    pred, kept, words, audio, gu_w = layer_forward(weights, glu_in, sizes, noisy, feats, words_in, flag)
    error = pred - target
    frame_n, chans = pred.shape
    mse = jnp.sum(error * error) / (frame_n * chans)
    d_pred = 2.0 * error / (frame_n * chans)
    audio_vec, pull_audio = jax.vjp(unit_scale, jnp.mean(audio, 0))
    text_vec, pull_text = jax.vjp(unit_scale, jnp.mean(words, 0))
    d_audio_vec, d_text_vec, con = contrast(audio_vec, text_vec, empty, negatives, sizes)
    weight = CON_WEIGHT * (1 - flag).astype(jnp.float32)
    d_audio_extra = pull_audio(d_audio_vec)[0][None, :] / frame_n
    d_words_extra = pull_text(d_text_vec)[0][None, :] / words.shape[0]
    lefts, rights, small = layer_backward(
        weights, gu_w, kept, words_in, d_pred, d_audio_extra, d_words_extra
    )
    loss_local = mse + weight * con
    bucket_local = (jnp.arange(NB, dtype=jnp.int32) == step_id).astype(jnp.float32) * mse
    line = jnp.concatenate([loss_local[None], jnp.zeros((1,), jnp.float32), bucket_local])
    line = jnp.pad(line[None], ((0, 7), (0, LANES - line.shape[0])))
    shares, sums = scatter_grads(lefts, rights, small, masters, line, sizes)
    loss_sum, total_sq, bucket_sums = sums[0], sums[1], sums[2 : 2 + NB]
    grad_norm = jnp.sqrt(total_sq)
    scale = jnp.minimum(1.0, CLIP_NORM / (grad_norm + 1e-06))
    new_weights, new_firsts, new_seconds = ([], [], [])
    for index, (master, first, second, share) in enumerate(zip(masters, firsts, seconds, shares)):
        rate = GAIN_RATE if index == len(masters) - 1 else RATE
        grad = share * scale
        first = BETA_ONE * first + (1.0 - BETA_ONE) * grad
        second = BETA_TWO * second + (1.0 - BETA_TWO) * grad * grad
        fixed_first = first / (1.0 - BETA_ONE**STEP)
        fixed_second = second / (1.0 - BETA_TWO**STEP)
        master = master - rate * (
            fixed_first / (jnp.sqrt(fixed_second) + ADAM_EPS) + DECAY * master
        )
        new_weights.append(master)
        new_firsts.append(first)
        new_seconds.append(second)
    return (
        loss_sum,
        bucket_sums,
        grad_norm,
        new_weights[0],
        new_weights[1],
        new_weights[2],
        new_weights[3],
        new_weights[4],
        new_weights[5],
        new_weights[6],
        new_weights[7],
        new_weights[8],
        new_firsts[0],
        new_firsts[1],
        new_firsts[2],
        new_firsts[3],
        new_firsts[4],
        new_firsts[5],
        new_firsts[6],
        new_firsts[7],
        new_firsts[8],
        new_seconds[0],
        new_seconds[1],
        new_seconds[2],
        new_seconds[3],
        new_seconds[4],
        new_seconds[5],
        new_seconds[6],
        new_seconds[7],
        new_seconds[8],
    )


def solution(mesh):
    sizes = (mesh.shape["dp"], mesh.shape["fsdp"])
    return jax.shard_map(
        functools.partial(body, sizes),
        mesh=mesh,
        in_specs=(
            P(("dp", "fsdp"), None, None),
            P(("dp", "fsdp"), None, None),
            P(("dp", "fsdp"), None, None),
            P(("dp", "fsdp")),
            P(("dp", "fsdp")),
            P(("dp", "fsdp"), None),
            P(None, ("dp", "fsdp")),
            P(("dp", "fsdp"), None),
            P(("dp", "fsdp"), None),
            P(("dp", "fsdp"), None),
            P(("dp", "fsdp"), None),
            P(("dp", "fsdp"), None),
            P(("dp", "fsdp"), None),
            P(("dp", "fsdp"), None),
            P(None, ("dp", "fsdp")),
            P(None, ("dp", "fsdp")),
            P(("dp", "fsdp"), None),
            P(("dp", "fsdp"), None),
            P(("dp", "fsdp"), None),
            P(("dp", "fsdp"), None),
            P(("dp", "fsdp"), None),
            P(("dp", "fsdp"), None),
            P(("dp", "fsdp"), None),
            P(None, ("dp", "fsdp")),
            P(None, ("dp", "fsdp")),
            P(("dp", "fsdp"), None),
            P(("dp", "fsdp"), None),
            P(("dp", "fsdp"), None),
            P(("dp", "fsdp"), None),
            P(("dp", "fsdp"), None),
            P(("dp", "fsdp"), None),
            P(("dp", "fsdp"), None),
            P(None, ("dp", "fsdp")),
        ),
        out_specs=(
            P(),
            P(),
            P(),
            P(None, ("dp", "fsdp")),
            P(("dp", "fsdp"), None),
            P(("dp", "fsdp"), None),
            P(("dp", "fsdp"), None),
            P(("dp", "fsdp"), None),
            P(("dp", "fsdp"), None),
            P(("dp", "fsdp"), None),
            P(("dp", "fsdp"), None),
            P(None, ("dp", "fsdp")),
            P(None, ("dp", "fsdp")),
            P(("dp", "fsdp"), None),
            P(("dp", "fsdp"), None),
            P(("dp", "fsdp"), None),
            P(("dp", "fsdp"), None),
            P(("dp", "fsdp"), None),
            P(("dp", "fsdp"), None),
            P(("dp", "fsdp"), None),
            P(None, ("dp", "fsdp")),
            P(None, ("dp", "fsdp")),
            P(("dp", "fsdp"), None),
            P(("dp", "fsdp"), None),
            P(("dp", "fsdp"), None),
            P(("dp", "fsdp"), None),
            P(("dp", "fsdp"), None),
            P(("dp", "fsdp"), None),
            P(("dp", "fsdp"), None),
            P(None, ("dp", "fsdp")),
        ),
        check_vma=False,
    )
```
